512 devices in a mesh: src: 64 (over z, x), tm: 8 (over y, core).
Axes of the slice: x: 4, y: 4, z: 16, core: 2. Of those that a mesh axis runs over, the one named last changes fastest.
Arguments:
- waveforms: bfloat16 [16, 2048, 8192], P('tm', 'src'), may hold values from -6 to 6
- scen_weights: bfloat16 [1024, 2048], P(None, 'src'), may hold values from -0.125 to 0.125
- rates: float32 [1024], replicated, may hold values from 0.1 to 4
- tile_cells: int32 [8192], replicated, may hold values from 0 to 8191, each once
- level_base: int32 [8192], P('src'), may hold values from 0 to 7
- wet_mask: int32 [8192], P('src'), may hold values 0 or 1
Outputs:
- hazard: float32 [16, 8192], P('tm', 'src')
The draws below stay inside these ranges and needn't reach their ends.
Inputs may be any that keep to these rules, and one draw needn't show every extreme that they name: `tile_cells`: each cell appears exactly once.
All inputs are finite; a program needn't handle non-finite values. No bound on the sum of `wet_mask` on one device may be relied on, other than what follows from the above.
Results may differ from the reference program's by a relative error of at most 0.0003.
Values may be sent and summed in bfloat16 or wider, within the bound.
No kernel may reach another device: no remote copies, remote signals or barrier semaphores. Data moves between devices by JAX's collectives and lax.ppermute only.
A program may use at most 64 MiB of HBM per device.

```python
import math
import jax
import jax.numpy as jnp
from jax import lax

S = 2048
C = 8192
TS = 16
K = 1024
NB = 16


def set_ends(entries, own_key, smallest, high):
    longest = entries.shape.index(max(entries.shape))
    spots = []
    for shift in (0, 1):
        where = [jax.random.randint(jax.random.fold_in(own_key, axis), (), 0, length) for axis, length in enumerate(entries.shape)]
        where[longest] = (where[longest] + shift) % entries.shape[longest]
        spots.append(tuple(where))
    return entries.at[spots[0]].set(smallest).at[spots[1]].set(high)


def block_levels(key, shape, pieces, low, high):
    level = 1.0
    for axis_at, blocks in pieces:
        steps = jax.random.uniform(jax.random.fold_in(jax.random.fold_in(key, 6), axis_at), (blocks,), jnp.float32, low / len(pieces), high / len(pieces))
        level = level * jnp.repeat(jnp.exp(steps), shape[axis_at] // blocks).reshape((-1,) + (1,) * (len(shape) - 1 - axis_at))
    return level


def normal_values(rng, dims, spread, reach, split=(), kind=jnp.bfloat16):
    entries = jax.random.normal(rng, dims, jnp.float32) * spread
    if len(split) > 0:
        entries = block_levels(rng, dims, split, -0.22, 0.18) * entries
    return jnp.clip(entries, min=-reach, max=reach).astype(kind)


def setup_inputs(seed: int = 0) -> dict:
    key_of = jax.random.split(jax.random.key(seed), 7)
    return {
        "waveforms": normal_values(key_of[0], (TS, S, C), 1.0, 6.0, ((0, 8), (1, 64))),
        "scen_weights": normal_values(key_of[1], (K, S), S ** -0.5, 0.125, ((1, 64),)),
        "rates": jnp.clip(jnp.exp(jax.random.uniform(key_of[2], (K,), jnp.float32, math.log(0.1), math.log(4.0))), 0.1, 4.0),
        "tile_cells": jax.random.permutation(key_of[3], C).astype(jnp.int32),
        "level_base": set_ends(jax.random.randint(key_of[4], (C,), 0, 8), jax.random.fold_in(key_of[4], 1), 0, 7).astype(jnp.int32),
        "wet_mask": set_ends((jax.random.randint(key_of[5], (C,), 0, 4) < 3).astype(jnp.int32), jax.random.fold_in(key_of[5], 1), 0, 1),
    }


def reference(waveforms, scen_weights, rates, tile_cells, level_base, wet_mask):
    tiled = jnp.take(waveforms, tile_cells, axis=2)

    def one_snap(carry, snap):
        value = jnp.dot(scen_weights, snap, preferred_element_type=jnp.float32)
        return (jnp.maximum(carry, value), 0)
    first = jnp.dot(scen_weights, tiled[0], preferred_element_type=jnp.float32)
    peak, unused = lax.scan(one_snap, first, tiled[1:])
    log_amp = jnp.log(jnp.maximum(peak, 0.1))
    base = level_base.astype(jnp.float32)
    scale = 1.0 / (0.5 * jnp.sqrt(jnp.float32(2.0)))

    def one_level(level):
        log_level = jnp.log(jnp.float32(0.1)) + 0.15 * (base + level.astype(jnp.float32))
        exceed = 0.5 * jax.scipy.special.erfc((log_level[None, :] - log_amp) * scale)
        return jnp.dot(rates, exceed, precision=lax.Precision.HIGHEST) / K
    hazard = lax.map(one_level, jnp.arange(NB, dtype=jnp.int32))
    return hazard * wet_mask.astype(jnp.float32)[None, :]
```

```python
import functools

import jax
import jax.numpy as jnp
from jax import lax
from jax.experimental import pallas as pl
from jax.experimental.pallas import tpu as pltpu
from jax.sharding import Mesh, PartitionSpec as P

K = 1024
NB = 16
C = 8192
EVERY = ("z", "x", "y", "c")
MIB = 1 << 20

ERFC_P = (
    2.326819970068386e-2,
    -1.387039388740657e-1,
    3.687424674597105e-1,
    -5.824733027278666e-1,
    6.210004621745983e-1,
    -4.944515323274145e-1,
    3.404879937665872e-1,
    -2.741127028184656e-1,
    5.638259427386472e-1,
)
ERFC_R = (
    -1.047766399936249e1,
    1.297719955372516e1,
    -7.495518717768503e0,
    2.921019019210786e0,
    -1.015265279202700e0,
    4.218463358204948e-1,
    -2.820767439740514e-1,
    5.641895067754075e-1,
)
ERF_T = (
    7.853861353153693e-5,
    -8.010193625184903e-4,
    5.188327685732524e-3,
    -2.685381193529856e-2,
    1.128358514861418e-1,
    -3.761262582423300e-1,
    1.128379165726710e0,
)


def poly(x, coefficients):
    total = jnp.full_like(x, coefficients[0])
    for c in coefficients[1:]:
        total = total * x + c
    return total


def erfc(x):
    square = x * x
    inner = 1.0 - x * poly(square, ERF_T)
    size = jnp.maximum(jnp.abs(x), 1.0)
    inverse = 1.0 / size
    q = inverse * inverse
    tail = jnp.exp(-square) * inverse * jnp.where(size < 2.0, poly(q, ERFC_P), poly(q, ERFC_R))
    outer = jnp.where(x < 0.0, 2.0 - tail, tail)
    return jnp.where(jnp.abs(x) < 1.0, inner, outer)


def gather_kernel(cells_ref, wave_ref, out_ref, turned, picked):
    half = C // 2

    @pl.loop(0, half // 128)
    def _(j):
        low = wave_ref[:, pl.ds(pl.multiple_of(j * 128, 128), 128)]
        high = wave_ref[:, pl.ds(pl.multiple_of(half + j * 128, 128), 128)]
        both = jnp.concatenate([low.astype(jnp.float32), high.astype(jnp.float32)], axis=0).T
        turned[pl.ds(pl.multiple_of(j * 128, 128), 128), :] = both
        turned[pl.ds(pl.multiple_of(half + j * 128, 128), 128), :] = pltpu.roll(both, 64, 1)

    first = lax.broadcasted_iota(jnp.int32, (1, 128), 1) < 64

    @pl.loop(0, C // 32)
    def _(pair):
        for e in range(2):
            for a in range(8):
                at = pair * 32 + e * 16 + a
                one = turned[pl.ds(cells_ref[at], 1), :]
                two = turned[pl.ds(cells_ref[at + 8] ^ half, 1), :]
                picked[pl.ds(pair * 16 + e * 8 + a, 1), :] = jnp.where(first, one, two)

    @pl.loop(0, C // 2 // 128)
    def _(i):
        rows = pl.ds(pl.multiple_of(i * 128, 128), 128)
        out_ref[rows, :] = picked[rows, :].astype(jnp.bfloat16)


def gather(cells, wave):
    return pl.pallas_call(
        gather_kernel,
        out_shape=jax.ShapeDtypeStruct((C // 2, 128), jnp.bfloat16),
        in_specs=[pl.BlockSpec(memory_space=pltpu.SMEM), pl.BlockSpec(memory_space=pltpu.VMEM)],
        out_specs=pl.BlockSpec(memory_space=pltpu.VMEM),
        scratch_shapes=[pltpu.VMEM((C, 128), jnp.float32), pltpu.VMEM((C // 2, 128), jnp.float32)],
        compiler_params=pltpu.CompilerParams(vmem_limit_bytes=32 * MIB),
        cost_estimate=pl.CostEstimate(flops=1 << 20, bytes_accessed=40 * MIB, transcendentals=0),
        name="gather_cells",
    )(cells, wave)


def hazard_kernel(got_ref, weights_ref, rates_ref, base_ref, out_ref, columns, weights, logs, sem):
    copy = pltpu.make_async_copy(weights_ref, weights, sem)
    copy.start()
    lane = lax.broadcasted_iota(jnp.int32, (16, 128), 1)
    in64 = lane < 64
    in32 = (lane & 63) < 32

    def swap(one, two, shift, mask):
        return (
            jnp.where(mask, one, pltpu.roll(two, shift, 1)),
            jnp.where(mask, pltpu.roll(one, 128 - shift, 1), two),
        )

    @pl.loop(0, 4)
    def _(x):
        for y in range(4):
            for zq in range(4):
                tiles = []
                for i in range(4):
                    row = (4 * zq + i) * 256 + x * 64 + y * 16
                    tiles.append(got_ref[pl.ds(pl.multiple_of(row, 16), 16), :].astype(jnp.float32))
                v0, v2 = swap(tiles[0], tiles[2], 64, in64)
                v1, v3 = swap(tiles[1], tiles[3], 64, in64)
                w0, w1 = swap(v0, v1, 32, in32)
                w2, w3 = swap(v2, v3, 32, in32)
                for c in range(2):
                    part = slice(8 * c, 8 * c + 8)
                    for t, (early, late) in enumerate(((w0, w2), (w1, w3))):
                        block = jnp.concatenate([early[part], late[part]], axis=0)
                        at = ((2 * y + c) * 2 + t) * 16
                        columns[at : at + 16, pl.ds(pl.multiple_of(x * 512 + zq * 128, 128), 128)] = block.astype(jnp.bfloat16)

    copy.wait()
    for n in range(4):
        total = jnp.zeros((256, 256), jnp.float32)
        for x in range(4):
            at = (x * 8 + 2 * n) * 512
            right = jnp.concatenate([weights[at : at + 512, :], weights[at + 512 : at + 1024, :]], axis=1)
            total += jnp.dot(columns[:, x * 512 : (x + 1) * 512], right, preferred_element_type=jnp.float32)
        peak = total[0:16]
        for t in range(1, 16):
            peak = jnp.maximum(peak, total[t * 16 : (t + 1) * 16])
        logs[:, n * 256 : (n + 1) * 256] = jnp.log(jnp.maximum(peak, 0.1))

    log_amp = logs[...]
    scale = 1.0 / (0.5 * jnp.sqrt(jnp.float32(2.0)))
    bottom = jnp.log(jnp.full((16, 128), 0.1, jnp.float32))
    rates = rates_ref[...]
    base = base_ref[...]

    def level(j, result):
        log_level = (bottom + 0.15 * (base + j.astype(jnp.float32)))[:, 0:1]
        value = rates * erfc((log_level - log_amp) * scale)
        hazard = jnp.sum(value, axis=1, keepdims=True) * (0.5 / K)
        return jnp.where(lane == j, hazard, result)

    out_ref[...] = lax.fori_loop(0, NB, level, jnp.zeros((16, 128), jnp.float32))


def hazard_of(got, weights, rates, base):
    vmem = pl.BlockSpec(memory_space=pltpu.VMEM)
    return pl.pallas_call(
        hazard_kernel,
        out_shape=jax.ShapeDtypeStruct((16, 128), jnp.float32),
        in_specs=[vmem, pl.BlockSpec(memory_space=pl.ANY), vmem, vmem],
        out_specs=vmem,
        scratch_shapes=[
            pltpu.VMEM((256, 2048), jnp.bfloat16),
            pltpu.VMEM((16384, 128), jnp.bfloat16),
            pltpu.VMEM((16, 1024), jnp.float32),
            pltpu.SemaphoreType.DMA,
        ],
        compiler_params=pltpu.CompilerParams(vmem_limit_bytes=32 * MIB),
        name="hazard_levels",
    )(got, weights, rates, base)


def body(waveforms, scen_weights, rates, tile_cells, level_base, wet_mask):
    me = lax.axis_index(("y", "c"))
    eighth = lax.dynamic_slice_in_dim(scen_weights.T, me * 128, 128, axis=1)
    shared = lax.all_to_all(jnp.broadcast_to(eighth[None], (16, 32, 128)), "z", 0, 0, tiled=True)
    sent = gather(tile_cells, waveforms.reshape(64, C))
    weights = lax.all_gather(shared.reshape(512, 128), ("x", "y", "c"), axis=0, tiled=True)
    got = lax.all_to_all(sent.reshape(512, 8, 128), EVERY, 0, 0, tiled=True)
    base = lax.dynamic_slice_in_dim(level_base.astype(jnp.float32), me * 16, 16)
    base = jnp.broadcast_to(base[:, None], (16, 128))
    part = hazard_of(got.reshape(C // 2, 128), weights, rates.reshape(1, K), base)
    levels = part[:, :NB].reshape(16, 8, 2).transpose(1, 2, 0)
    hazard = lax.all_to_all(levels, ("y", "c"), 0, 0, tiled=True).transpose(1, 0, 2).reshape(2, 128)
    return hazard * wet_mask.astype(jnp.float32)[None, :]


def solution(mesh):
    split = Mesh(mesh.devices.reshape(16, 4, 4, 2), EVERY)
    src, tm = ("z", "x"), ("y", "c")
    return jax.shard_map(
        body,
        mesh=split,
        in_specs=(P(tm, src, None), P(None, src), P(), P(), P(src), P(src)),
        out_specs=P(tm, src),
        check_vma=False,
    )
```

```python
import functools

import jax
import jax.numpy as jnp
from jax import lax
from jax.experimental import pallas as pl
from jax.experimental.pallas import tpu as pltpu
from jax.sharding import Mesh, PartitionSpec as P

K = 1024
NB = 16
C = 8192
EVERY = ("z", "x", "y", "c")
MIB = 1 << 20

ERFC_P = (
    2.326819970068386e-2,
    -1.387039388740657e-1,
    3.687424674597105e-1,
    -5.824733027278666e-1,
    6.210004621745983e-1,
    -4.944515323274145e-1,
    3.404879937665872e-1,
    -2.741127028184656e-1,
    5.638259427386472e-1,
)
ERFC_R = (
    -1.047766399936249e1,
    1.297719955372516e1,
    -7.495518717768503e0,
    2.921019019210786e0,
    -1.015265279202700e0,
    4.218463358204948e-1,
    -2.820767439740514e-1,
    5.641895067754075e-1,
)
ERF_T = (
    7.853861353153693e-5,
    -8.010193625184903e-4,
    5.188327685732524e-3,
    -2.685381193529856e-2,
    1.128358514861418e-1,
    -3.761262582423300e-1,
    1.128379165726710e0,
)


def poly(x, coefficients):
    total = jnp.full_like(x, coefficients[0])
    for c in coefficients[1:]:
        total = total * x + c
    return total


def erfc(x):
    square = x * x
    inner = 1.0 - x * poly(square, ERF_T)
    size = jnp.maximum(jnp.abs(x), 1.0)
    inverse = 1.0 / size
    q = inverse * inverse
    tail = jnp.exp(-square) * inverse * jnp.where(size < 2.0, poly(q, ERFC_P), poly(q, ERFC_R))
    outer = jnp.where(x < 0.0, 2.0 - tail, tail)
    return jnp.where(jnp.abs(x) < 1.0, inner, outer)


def gather_kernel(cells_ref, wave_ref, out_ref, turned, picked):
    half = C // 2

    @pl.loop(0, half // 128)
    def _(j):
        low = wave_ref[:, pl.ds(pl.multiple_of(j * 128, 128), 128)]
        high = wave_ref[:, pl.ds(pl.multiple_of(half + j * 128, 128), 128)]
        both = jnp.concatenate([low.astype(jnp.float32), high.astype(jnp.float32)], axis=0).T
        turned[pl.ds(pl.multiple_of(j * 128, 128), 128), :] = both
        turned[pl.ds(pl.multiple_of(half + j * 128, 128), 128), :] = pltpu.roll(both, 64, 1)

    first = lax.broadcasted_iota(jnp.int32, (1, 128), 1) < 64

    @pl.loop(0, C // 32)
    def _(pair):
        for e in range(2):
            for a in range(8):
                at = pair * 32 + e * 16 + a
                one = turned[pl.ds(cells_ref[at], 1), :]
                two = turned[pl.ds(cells_ref[at + 8] ^ half, 1), :]
                picked[pl.ds(pair * 16 + e * 8 + a, 1), :] = jnp.where(first, one, two)

    @pl.loop(0, C // 2 // 128)
    def _(i):
        rows = pl.ds(pl.multiple_of(i * 128, 128), 128)
        out_ref[rows, :] = picked[rows, :].astype(jnp.bfloat16)


def gather(cells, wave):
    return pl.pallas_call(
        gather_kernel,
        out_shape=jax.ShapeDtypeStruct((C // 2, 128), jnp.bfloat16),
        in_specs=[pl.BlockSpec(memory_space=pltpu.SMEM), pl.BlockSpec(memory_space=pltpu.VMEM)],
        out_specs=pl.BlockSpec(memory_space=pltpu.VMEM),
        scratch_shapes=[pltpu.VMEM((C, 128), jnp.float32), pltpu.VMEM((C // 2, 128), jnp.float32)],
        compiler_params=pltpu.CompilerParams(vmem_limit_bytes=32 * MIB),
        cost_estimate=pl.CostEstimate(flops=1 << 20, bytes_accessed=40 * MIB, transcendentals=0),
        name="gather_cells",
    )(cells, wave)


def hazard_kernel(got_ref, weights_ref, rates_ref, base_ref, out_ref, columns, weights, logs, sem):
    copy = pltpu.make_async_copy(weights_ref, weights, sem)
    copy.start()
    lane = lax.broadcasted_iota(jnp.int32, (16, 128), 1)
    in64 = lane < 64
    in32 = (lane & 63) < 32

    def swap(one, two, shift, mask):
        return (
            jnp.where(mask, one, pltpu.roll(two, shift, 1)),
            jnp.where(mask, pltpu.roll(one, 128 - shift, 1), two),
        )

    @pl.loop(0, 4)
    def _(x):
        for y in range(4):
            for zq in range(4):
                tiles = []
                for i in range(4):
                    row = (4 * zq + i) * 256 + x * 64 + y * 16
                    tiles.append(got_ref[pl.ds(pl.multiple_of(row, 16), 16), :].astype(jnp.float32))
                v0, v2 = swap(tiles[0], tiles[2], 64, in64)
                v1, v3 = swap(tiles[1], tiles[3], 64, in64)
                w0, w1 = swap(v0, v1, 32, in32)
                w2, w3 = swap(v2, v3, 32, in32)
                for c in range(2):
                    part = slice(8 * c, 8 * c + 8)
                    for t, (early, late) in enumerate(((w0, w2), (w1, w3))):
                        block = jnp.concatenate([early[part], late[part]], axis=0)
                        at = ((2 * y + c) * 2 + t) * 16
                        columns[at : at + 16, pl.ds(pl.multiple_of(x * 512 + zq * 128, 128), 128)] = block.astype(jnp.bfloat16)

    copy.wait()
    for n in range(4):
        total = jnp.zeros((256, 256), jnp.float32)
        for x in range(4):
            at = (x * 8 + 2 * n) * 512
            right = jnp.concatenate([weights[at : at + 512, :], weights[at + 512 : at + 1024, :]], axis=1)
            total += jnp.dot(columns[:, x * 512 : (x + 1) * 512], right, preferred_element_type=jnp.float32)
        peak = total[0:16]
        for t in range(1, 16):
            peak = jnp.maximum(peak, total[t * 16 : (t + 1) * 16])
        logs[:, n * 256 : (n + 1) * 256] = jnp.log(jnp.maximum(peak, 0.1))

    log_amp = logs[...]
    scale = 1.0 / (0.5 * jnp.sqrt(jnp.float32(2.0)))
    bottom = jnp.log(jnp.full((16, 128), 0.1, jnp.float32))
    rates = rates_ref[...]
    base = base_ref[...]

    def level(j, result):
        log_level = (bottom + 0.15 * (base + j.astype(jnp.float32)))[:, 0:1]
        value = rates * erfc((log_level - log_amp) * scale)
        hazard = jnp.sum(value, axis=1, keepdims=True) * (0.5 / K)
        return jnp.where(lane == j, hazard, result)

    out_ref[...] = lax.fori_loop(0, NB, level, jnp.zeros((16, 128), jnp.float32))


def hazard_of(got, weights, rates, base):
    vmem = pl.BlockSpec(memory_space=pltpu.VMEM)
    return pl.pallas_call(
        hazard_kernel,
        out_shape=jax.ShapeDtypeStruct((16, 128), jnp.float32),
        in_specs=[vmem, pl.BlockSpec(memory_space=pl.ANY), vmem, vmem],
        out_specs=vmem,
        scratch_shapes=[
            pltpu.VMEM((256, 2048), jnp.bfloat16),
            pltpu.VMEM((16384, 128), jnp.bfloat16),
            pltpu.VMEM((16, 1024), jnp.float32),
            pltpu.SemaphoreType.DMA,
        ],
        compiler_params=pltpu.CompilerParams(vmem_limit_bytes=32 * MIB),
        name="hazard_levels",
    )(got, weights, rates, base)


def body(waveforms, scen_weights, rates, tile_cells, level_base, wet_mask):
    me = lax.axis_index(("y", "c"))
    eighth = lax.dynamic_slice_in_dim(scen_weights.T, me * 128, 128, axis=1)
    shared = lax.all_to_all(jnp.broadcast_to(eighth[None], (16, 32, 128)), "z", 0, 0, tiled=True)
    shared, sent = lax.optimization_barrier((shared, gather(tile_cells, waveforms.reshape(64, C))))
    weights = lax.all_gather(shared.reshape(512, 128), ("x", "y", "c"), axis=0, tiled=True)
    got = lax.all_to_all(sent.reshape(512, 8, 128), EVERY, 0, 0, tiled=True)
    base = lax.dynamic_slice_in_dim(level_base.astype(jnp.float32), me * 16, 16)
    base = jnp.broadcast_to(base[:, None], (16, 128))
    part = hazard_of(got.reshape(C // 2, 128), weights, rates.reshape(1, K), base)
    levels = part[:, :NB].reshape(16, 8, 2).transpose(1, 2, 0)
    hazard = lax.all_to_all(levels, ("y", "c"), 0, 0, tiled=True).transpose(1, 0, 2).reshape(2, 128)
    return hazard * wet_mask.astype(jnp.float32)[None, :]


def solution(mesh):
    split = Mesh(mesh.devices.reshape(16, 4, 4, 2), EVERY)
    src, tm = ("z", "x"), ("y", "c")
    return jax.shard_map(
        body,
        mesh=split,
        in_specs=(P(tm, src, None), P(None, src), P(), P(), P(src), P(src)),
        out_specs=P(tm, src),
        check_vma=False,
    )
```

```python
import functools

import jax
import jax.numpy as jnp
from jax import lax
from jax.experimental import pallas as pl
from jax.experimental.pallas import tpu as pltpu
from jax.sharding import Mesh, PartitionSpec as P

K = 1024
NB = 16
C = 8192
EVERY = ("z", "x", "y", "c")
MIB = 1 << 20

ERFC = (
    0.17087277,
    -0.82215223,
    1.48851587,
    -1.13520398,
    0.27886807,
    -0.18628806,
    0.09678418,
    0.37409196,
    1.00002368,
    -1.26551223,
)


def erfc(x):
    size = jnp.abs(x)
    t = 1.0 / (1.0 + 0.5 * size)
    total = jnp.full_like(t, ERFC[0])
    for c in ERFC[1:]:
        total = total * t + c
    tail = t * jnp.exp(total - x * x)
    return jnp.where(x < 0.0, 2.0 - tail, tail)


def gather_kernel(cells_ref, wave_ref, out_ref, turned, picked):
    half = C // 2

    @pl.loop(0, half // 128)
    def _(j):
        low = wave_ref[:, pl.ds(pl.multiple_of(j * 128, 128), 128)]
        high = wave_ref[:, pl.ds(pl.multiple_of(half + j * 128, 128), 128)]
        one = jnp.concatenate([low, high], axis=0).T.astype(jnp.float32)
        two = jnp.concatenate([high, low], axis=0).T.astype(jnp.float32)
        turned[pl.ds(pl.multiple_of(j * 128, 128), 128), :] = one
        turned[pl.ds(pl.multiple_of(half + j * 128, 128), 128), :] = two
        turned[pl.ds(pl.multiple_of(C + j * 128, 128), 128), :] = one

    first = lax.broadcasted_iota(jnp.int32, (1, 128), 1) < 64

    @pl.loop(0, C // 64)
    def _(four):
        for e in range(4):
            for a in range(8):
                at = four * 64 + e * 16 + a
                one = turned[pl.ds(cells_ref[at], 1), :]
                two = turned[pl.ds(cells_ref[at + 8] + half, 1), :]
                picked[pl.ds(four * 32 + e * 8 + a, 1), :] = jnp.where(first, one, two)

    @pl.loop(0, C // 2 // 128)
    def _(i):
        rows = pl.ds(pl.multiple_of(i * 128, 128), 128)
        out_ref[rows, :] = picked[rows, :].astype(jnp.bfloat16)


def gather(cells, wave):
    return pl.pallas_call(
        gather_kernel,
        out_shape=jax.ShapeDtypeStruct((C // 2, 128), jnp.bfloat16),
        in_specs=[pl.BlockSpec(memory_space=pltpu.SMEM), pl.BlockSpec(memory_space=pltpu.VMEM)],
        out_specs=pl.BlockSpec(memory_space=pltpu.VMEM),
        scratch_shapes=[pltpu.VMEM((C + C // 2, 128), jnp.float32), pltpu.VMEM((C // 2, 128), jnp.float32)],
        compiler_params=pltpu.CompilerParams(vmem_limit_bytes=60 * MIB),
        cost_estimate=pl.CostEstimate(flops=1 << 20, bytes_accessed=40 * MIB, transcendentals=0),
        name="gather_cells",
    )(cells, wave)


def hazard_kernel(me_ref, got_ref, weights_ref, rates_ref, base_ref, wet_ref, out_ref, columns, weights, logs, sums, sem):
    copy = pltpu.make_async_copy(weights_ref, weights, sem)
    copy.start()
    scale = 1.0 / (0.5 * jnp.sqrt(jnp.float32(2.0)))
    lane = lax.broadcasted_iota(jnp.int32, (16, 128), 1)
    in64 = lane < 64
    in32 = (lane & 63) < 32

    def swap(one, two, shift, mask):
        return (
            jnp.where(mask, one, pltpu.roll(two, shift, 1)),
            jnp.where(mask, pltpu.roll(one, 128 - shift, 1), two),
        )

    @pl.loop(0, 4)
    def _(x):
        for y in range(4):
            for zq in range(4):
                tiles = []
                for i in range(4):
                    row = (4 * zq + i) * 256 + x * 64 + y * 16
                    tiles.append(got_ref[pl.ds(pl.multiple_of(row, 16), 16), :].astype(jnp.float32))
                v0, v2 = swap(tiles[0], tiles[2], 64, in64)
                v1, v3 = swap(tiles[1], tiles[3], 64, in64)
                w0, w1 = swap(v0, v1, 32, in32)
                w2, w3 = swap(v2, v3, 32, in32)
                for c in range(2):
                    part = slice(8 * c, 8 * c + 8)
                    for t, (early, late) in enumerate(((w0, w2), (w1, w3))):
                        block = jnp.concatenate([early[part], late[part]], axis=0)
                        at = ((2 * y + c) * 2 + t) * 16
                        columns[at : at + 16, pl.ds(pl.multiple_of(x * 512 + zq * 128, 128), 128)] = block.astype(jnp.bfloat16)

    copy.wait()
    for n in range(4):
        total = jnp.zeros((256, 256), jnp.float32)
        for x in range(4):
            at = (x * 8 + 2 * n) * 512
            right = jnp.concatenate([weights[at : at + 512, :], weights[at + 512 : at + 1024, :]], axis=1)
            total += jnp.dot(columns[:, x * 512 : (x + 1) * 512], right, preferred_element_type=jnp.float32)
        peak = total[0:16]
        for t in range(1, 16):
            peak = jnp.maximum(peak, total[t * 16 : (t + 1) * 16])
        logs[:, n * 256 : (n + 1) * 256] = jnp.log(jnp.maximum(peak, 0.1))

    row = lax.broadcasted_iota(jnp.int32, (16, 128), 0)
    mine = lane == me_ref[0] * 16 + row
    base = jnp.sum(jnp.where(mine, base_ref[...].astype(jnp.float32), 0.0), axis=1, keepdims=True)
    wet = wet_ref[...].astype(jnp.float32)
    bottom = jnp.log(jnp.full((16, 1), 0.1, jnp.float32))

    @pl.loop(0, NB)
    def _(j):
        log_level = jnp.broadcast_to(bottom + 0.15 * (base + j.astype(jnp.float32)), (16, 128))
        total = jnp.zeros((16, 128), jnp.float32)
        for b in range(8):
            part = slice(b * 128, b * 128 + 128)
            total += rates_ref[:, part] * erfc((log_level - logs[:, part]) * scale)
        sums[pl.ds(pl.multiple_of(j * 16, 16), 16), :] = total

    for j in range(NB):
        hazard = jnp.sum(sums[j * 16 : j * 16 + 16, :], axis=1, keepdims=True) * (0.5 / K)
        out_ref[j : j + 1, :] = jnp.sum(jnp.where(mine, hazard, 0.0), axis=0, keepdims=True) * wet


def hazard_of(me, got, weights, rates, base, wet):
    vmem = pl.BlockSpec(memory_space=pltpu.VMEM)
    return pl.pallas_call(
        hazard_kernel,
        out_shape=jax.ShapeDtypeStruct((16, 128), jnp.float32),
        in_specs=[pl.BlockSpec(memory_space=pltpu.SMEM), vmem, pl.BlockSpec(memory_space=pl.ANY), vmem, vmem, vmem],
        out_specs=vmem,
        scratch_shapes=[
            pltpu.VMEM((256, 2048), jnp.bfloat16),
            pltpu.VMEM((16384, 128), jnp.bfloat16),
            pltpu.VMEM((16, 1024), jnp.float32),
            pltpu.VMEM((256, 128), jnp.float32),
            pltpu.SemaphoreType.DMA,
        ],
        compiler_params=pltpu.CompilerParams(vmem_limit_bytes=58 * MIB),
        name="hazard_levels",
    )(me, got, weights, rates, base, wet)


def body(waveforms, scen_weights, rates, tile_cells, level_base, wet_mask):
    me = lax.axis_index(("y", "c"))
    eighth = lax.dynamic_slice_in_dim(scen_weights.T, me * 128, 128, axis=1)
    shared = lax.all_to_all(jnp.broadcast_to(eighth[None], (16, 32, 128)), "z", 0, 0, tiled=True)
    shared, sent = lax.optimization_barrier((shared, gather(tile_cells, waveforms.reshape(64, C))))
    weights = lax.all_gather(shared.reshape(512, 128), ("x", "y", "c"), axis=0, tiled=True)
    got = lax.all_to_all(sent.reshape(512, 8, 128), EVERY, 0, 0, tiled=True)
    part = hazard_of(
        me.reshape(1),
        got.reshape(C // 2, 128),
        weights,
        rates.reshape(1, K),
        level_base.reshape(1, 128),
        wet_mask.reshape(1, 128),
    )
    hazard = lax.all_to_all(part.reshape(8, 2, 128), ("y", "c"), 0, 0, tiled=True)
    return jnp.sum(hazard, axis=0)


def solution(mesh):
    split = Mesh(mesh.devices.reshape(16, 4, 4, 2), EVERY)
    src, tm = ("z", "x"), ("y", "c")
    return jax.shard_map(
        body,
        mesh=split,
        in_specs=(P(tm, src, None), P(None, src), P(), P(), P(src), P(src)),
        out_specs=P(tm, src),
        check_vma=False,
    )
```

```python
import functools

import jax
import jax.numpy as jnp
from jax import lax
from jax.experimental import pallas as pl
from jax.experimental.pallas import tpu as pltpu
from jax.sharding import Mesh, PartitionSpec as P

K = 1024
NB = 16
C = 8192
EVERY = ("z", "x", "y", "c")
MIB = 1 << 20
NEAR = (0, 1, 15, 2, 14, 3, 13, 4)
FAR = (12, 5, 11, 6, 10, 7, 9, 8)

ERFC = (
    0.17087277,
    -0.82215223,
    1.48851587,
    -1.13520398,
    0.27886807,
    -0.18628806,
    0.09678418,
    0.37409196,
    1.00002368,
    -1.26551223,
)


def erfc(x):
    size = jnp.abs(x)
    t = 1.0 / (1.0 + 0.5 * size)
    total = jnp.full_like(t, ERFC[0])
    for c in ERFC[1:]:
        total = total * t + c
    tail = t * jnp.exp(total - x * x)
    return jnp.where(x < 0.0, 2.0 - tail, tail)


def gather_kernel(cells_hbm, wave_hbm, out_hbm, cells, wave, turned, picked, out, cells_sem, wave_sem, out_sem):
    half, part = C // 2, C // 8
    cells_copy = pltpu.make_async_copy(cells_hbm, cells, cells_sem)
    loads = []
    for k in range(4):
        for h in range(2):
            lanes = slice(h * half + k * part, h * half + (k + 1) * part)
            loads.append(pltpu.make_async_copy(wave_hbm.at[:, lanes], wave.at[:, lanes], wave_sem.at[2 * k + h]))
    for copy in loads[:2] + [cells_copy] + loads[2:]:
        copy.start()

    for k in range(4):
        loads[2 * k].wait()
        loads[2 * k + 1].wait()

        @pl.loop(k * part // 128, (k + 1) * part // 128)
        def _(j):
            low = wave[:, pl.ds(pl.multiple_of(j * 128, 128), 128)]
            high = wave[:, pl.ds(pl.multiple_of(half + j * 128, 128), 128)]
            one = jnp.concatenate([low, high], axis=0).T.astype(jnp.float32)
            two = jnp.concatenate([high, low], axis=0).T.astype(jnp.float32)
            turned[pl.ds(pl.multiple_of(j * 128, 128), 128), :] = one
            turned[pl.ds(pl.multiple_of(half + j * 128, 128), 128), :] = two
            turned[pl.ds(pl.multiple_of(C + j * 128, 128), 128), :] = one

    cells_copy.wait()
    first = lax.broadcasted_iota(jnp.int32, (1, 128), 1) < 64
    stores = []
    for k in range(4):

        @pl.loop(k * C // 256, (k + 1) * C // 256)
        def _(four):
            for e in range(4):
                for a in range(8):
                    at = four * 64 + e * 16 + a
                    one = turned[pl.ds(cells[at], 1), :]
                    two = turned[pl.ds(cells[at + 8] + half, 1), :]
                    picked[pl.ds(four * 32 + e * 8 + a, 1), :] = jnp.where(first, one, two)

        @pl.loop(k * part // 128, (k + 1) * part // 128)
        def _(i):
            rows = pl.ds(pl.multiple_of(i * 128, 128), 128)
            out[rows, :] = picked[rows, :].astype(jnp.bfloat16)

        rows = slice(k * part, (k + 1) * part)
        stores.append(pltpu.make_async_copy(out.at[rows], out_hbm.at[rows], out_sem.at[k]))
        stores[k].start()
    for copy in stores:
        copy.wait()


def gather(cells, wave):
    hbm = pl.BlockSpec(memory_space=pl.ANY)
    return pl.pallas_call(
        gather_kernel,
        out_shape=jax.ShapeDtypeStruct((C // 2, 128), jnp.bfloat16),
        in_specs=[hbm, hbm],
        out_specs=hbm,
        scratch_shapes=[
            pltpu.SMEM((C,), jnp.int32),
            pltpu.VMEM((64, C), jnp.bfloat16),
            pltpu.VMEM((C + C // 2, 128), jnp.float32),
            pltpu.VMEM((C // 2, 128), jnp.float32),
            pltpu.VMEM((C // 2, 128), jnp.bfloat16),
            pltpu.SemaphoreType.DMA,
            pltpu.SemaphoreType.DMA((8,)),
            pltpu.SemaphoreType.DMA((4,)),
        ],
        compiler_params=pltpu.CompilerParams(vmem_limit_bytes=60 * MIB),
        cost_estimate=pl.CostEstimate(flops=1 << 20, bytes_accessed=40 * MIB, transcendentals=0),
        name="gather_cells",
    )(cells, wave)


def hazard_kernel(me_ref, got_ref, weights_ref, rates_ref, base_ref, wet_ref, out_ref, columns, weights, logs, sums, sem):
    copy = pltpu.make_async_copy(weights_ref, weights, sem)
    copy.start()
    scale = 1.0 / (0.5 * jnp.sqrt(jnp.float32(2.0)))
    lane = lax.broadcasted_iota(jnp.int32, (16, 128), 1)
    starts = []
    for near, far in zip(NEAR, FAR):
        for ahead in (near, far):
            starts.append(((me_ref[1] + ahead) & 15) * 256)

    to = lax.broadcasted_iota(jnp.int32, (1, 512), 1)
    source = ((to >> 5) & 3) * 128 + (to >> 7) * 32 + (to & 31)
    swap = (lax.broadcasted_iota(jnp.int32, (512, 512), 0) == source).astype(jnp.float32).astype(jnp.bfloat16)

    for x in range(4):
        tiles = []
        for y in range(4):
            for zq in range(4):
                rows = [pl.ds(pl.multiple_of(starts[4 * zq + i] + x * 64 + y * 16, 16), 16) for i in range(4)]
                tiles.append(jnp.concatenate([got_ref[row, :] for row in rows], axis=1))
        moved = jnp.dot(jnp.concatenate(tiles, axis=0), swap, preferred_element_type=jnp.float32)
        for y in range(4):
            for zq in range(4):
                at = (y * 4 + zq) * 16
                lanes = slice(x * 512 + zq * 128, x * 512 + zq * 128 + 128)
                for c in range(2):
                    part = moved[at + 8 * c : at + 8 * c + 8]
                    for t in range(2):
                        early, late = part[:, t * 128 : t * 128 + 128], part[:, 256 + t * 128 : 384 + t * 128]
                        to_row = ((2 * y + c) * 2 + t) * 16
                        columns[to_row : to_row + 16, lanes] = jnp.concatenate([early, late], axis=0).astype(jnp.bfloat16)

    copy.wait()
    for n in range(4):
        total = jnp.dot(columns[...], weights[:, n * 256 : (n + 1) * 256], preferred_element_type=jnp.float32)
        peak = total[0:16]
        for t in range(1, 16):
            peak = jnp.maximum(peak, total[t * 16 : (t + 1) * 16])
        logs[:, n * 256 : (n + 1) * 256] = jnp.log(jnp.maximum(peak, 0.1))

    row = lax.broadcasted_iota(jnp.int32, (16, 128), 0)
    mine = lane == me_ref[0] * 16 + row
    base = jnp.sum(jnp.where(mine, base_ref[...].astype(jnp.float32), 0.0), axis=1, keepdims=True)
    wet = wet_ref[...].astype(jnp.float32)
    bottom = jnp.log(jnp.full((16, 1), 0.1, jnp.float32))

    @pl.loop(0, NB)
    def _(j):
        log_level = jnp.broadcast_to(bottom + 0.15 * (base + j.astype(jnp.float32)), (16, 128))
        total = jnp.zeros((16, 128), jnp.float32)
        for b in range(8):
            part = slice(b * 128, b * 128 + 128)
            total += rates_ref[:, part] * erfc((log_level - logs[:, part]) * scale)
        sums[pl.ds(pl.multiple_of(j * 16, 16), 16), :] = total

    for j in range(NB):
        hazard = jnp.sum(sums[j * 16 : j * 16 + 16, :], axis=1, keepdims=True) * (0.5 / K)
        out_ref[j : j + 1, :] = jnp.sum(jnp.where(mine, hazard, 0.0), axis=0, keepdims=True) * wet


def hazard_of(me, got, weights, rates, base, wet):
    vmem = pl.BlockSpec(memory_space=pltpu.VMEM)
    return pl.pallas_call(
        hazard_kernel,
        out_shape=jax.ShapeDtypeStruct((16, 128), jnp.float32),
        in_specs=[pl.BlockSpec(memory_space=pltpu.SMEM), vmem, pl.BlockSpec(memory_space=pl.ANY), vmem, vmem, vmem],
        out_specs=vmem,
        scratch_shapes=[
            pltpu.VMEM((256, 2048), jnp.bfloat16),
            pltpu.VMEM((2048, K), jnp.bfloat16),
            pltpu.VMEM((16, 1024), jnp.float32),
            pltpu.VMEM((256, 128), jnp.float32),
            pltpu.SemaphoreType.DMA,
        ],
        compiler_params=pltpu.CompilerParams(vmem_limit_bytes=52 * MIB),
        name="hazard_levels",
    )(me, got, weights, rates, base, wet)


def body(waveforms, scen_weights, rates, tile_cells, level_base, wet_mask):
    me, z = lax.axis_index(("y", "c")), lax.axis_index("z")

    def fetch(steps):
        ring = [(((i + steps[r]) % 16) * 8 + r, i * 8 + r) for i in range(16) for r in range(8)]
        return lax.ppermute(scen_weights.T, ("z", "y", "c"), ring)

    far, near = fetch(FAR), fetch(NEAR)
    far, near, sent = lax.optimization_barrier((far, near, gather(tile_cells, waveforms.reshape(64, C))))
    weights = lax.all_gather(jnp.concatenate([near, far], axis=0), ("x", "y", "c"), axis=0, tiled=True)
    got = lax.all_to_all(sent.reshape(512, 8, 128), EVERY, 0, 0, tiled=True)
    part = hazard_of(
        jnp.stack([me, z]),
        got.reshape(C // 2, 128),
        weights,
        rates.reshape(1, K),
        level_base.reshape(1, 128),
        wet_mask.reshape(1, 128),
    )
    hazard = lax.all_to_all(part.reshape(8, 2, 128), ("y", "c"), 0, 0, tiled=True)
    return jnp.sum(hazard, axis=0)


def solution(mesh):
    split = Mesh(mesh.devices.reshape(16, 4, 4, 2), EVERY)
    src, tm = ("z", "x"), ("y", "c")
    return jax.shard_map(
        body,
        mesh=split,
        in_specs=(P(tm, src, None), P(None, src), P(), P(), P(src), P(src)),
        out_specs=P(tm, src),
        check_vma=False,
    )
```

```python
import functools

import jax
import jax.numpy as jnp
from jax import lax
from jax.experimental import pallas as pl
from jax.experimental.pallas import tpu as pltpu
from jax.sharding import Mesh, PartitionSpec as P

K = 1024
NB = 16
C = 8192
EVERY = ("z", "x", "y", "c")
MIB = 1 << 20
NEAR = (0, 1, 15, 2, 14, 3, 13, 4)
FAR = (12, 5, 11, 6, 10, 7, 9, 8)

ERFC = (
    0.17087277,
    -0.82215223,
    1.48851587,
    -1.13520398,
    0.27886807,
    -0.18628806,
    0.09678418,
    0.37409196,
    1.00002368,
    -1.26551223,
)


def erfc(x):
    size = jnp.abs(x)
    t = 1.0 / (1.0 + 0.5 * size)
    total = jnp.full_like(t, ERFC[0])
    for c in ERFC[1:]:
        total = total * t + c
    tail = t * jnp.exp(total - x * x)
    return jnp.where(x < 0.0, 2.0 - tail, tail)


def gather_kernel(cells_hbm, wave_hbm, out_hbm, cells, wave, turned, picked, out, cells_sem, wave_sem, out_sem):
    half, part = C // 2, C // 8
    cells_copy = pltpu.make_async_copy(cells_hbm, cells, cells_sem)
    loads = []
    for k in range(4):
        for h in range(2):
            lanes = slice(h * half + k * part, h * half + (k + 1) * part)
            loads.append(pltpu.make_async_copy(wave_hbm.at[:, lanes], wave.at[:, lanes], wave_sem.at[2 * k + h]))
    for copy in loads[:2] + [cells_copy] + loads[2:]:
        copy.start()

    for k in range(4):
        loads[2 * k].wait()
        loads[2 * k + 1].wait()

        @pl.loop(k * part // 128, (k + 1) * part // 128)
        def _(j):
            low = wave[:, pl.ds(pl.multiple_of(j * 128, 128), 128)]
            high = wave[:, pl.ds(pl.multiple_of(half + j * 128, 128), 128)]
            one = jnp.concatenate([low, high], axis=0).T.astype(jnp.float32)
            two = jnp.concatenate([high, low], axis=0).T.astype(jnp.float32)
            turned[pl.ds(pl.multiple_of(j * 128, 128), 128), :] = one
            turned[pl.ds(pl.multiple_of(half + j * 128, 128), 128), :] = two
            turned[pl.ds(pl.multiple_of(C + j * 128, 128), 128), :] = one

    cells_copy.wait()
    first = lax.broadcasted_iota(jnp.int32, (1, 128), 1) < 64
    stores = []
    for k in range(4):

        @pl.loop(k * C // 256, (k + 1) * C // 256)
        def _(four):
            for e in range(4):
                for a in range(8):
                    at = four * 64 + e * 16 + a
                    one = turned[pl.ds(cells[at], 1), :]
                    two = turned[pl.ds(cells[at + 8] + half, 1), :]
                    picked[pl.ds(four * 32 + e * 8 + a, 1), :] = jnp.where(first, one, two)

        @pl.loop(k * part // 128, (k + 1) * part // 128)
        def _(i):
            rows = pl.ds(pl.multiple_of(i * 128, 128), 128)
            out[rows, :] = picked[rows, :].astype(jnp.bfloat16)

        rows = slice(k * part, (k + 1) * part)
        stores.append(pltpu.make_async_copy(out.at[rows], out_hbm.at[rows], out_sem.at[k]))
        stores[k].start()
    for copy in stores:
        copy.wait()


def gather(cells, wave):
    hbm = pl.BlockSpec(memory_space=pl.ANY)
    return pl.pallas_call(
        gather_kernel,
        out_shape=jax.ShapeDtypeStruct((C // 2, 128), jnp.bfloat16),
        in_specs=[hbm, hbm],
        out_specs=hbm,
        scratch_shapes=[
            pltpu.SMEM((C,), jnp.int32),
            pltpu.VMEM((64, C), jnp.bfloat16),
            pltpu.VMEM((C + C // 2, 128), jnp.float32),
            pltpu.VMEM((C // 2, 128), jnp.float32),
            pltpu.VMEM((C // 2, 128), jnp.bfloat16),
            pltpu.SemaphoreType.DMA,
            pltpu.SemaphoreType.DMA((8,)),
            pltpu.SemaphoreType.DMA((4,)),
        ],
        compiler_params=pltpu.CompilerParams(vmem_limit_bytes=60 * MIB),
        cost_estimate=pl.CostEstimate(flops=1 << 20, bytes_accessed=40 * MIB, transcendentals=0),
        name="gather_cells",
    )(cells, wave)


def hazard_kernel(me_ref, got_ref, weights_ref, rates_ref, base_ref, wet_ref, out_ref, columns, weights, logs, sums, sem):
    copy = pltpu.make_async_copy(weights_ref, weights, sem)
    copy.start()
    scale = 1.0 / (0.5 * jnp.sqrt(jnp.float32(2.0)))
    lane = lax.broadcasted_iota(jnp.int32, (16, 128), 1)
    starts = []
    for near, far in zip(NEAR, FAR):
        for ahead in (far, near):
            starts.append(((me_ref[1] + ahead) & 15) * 256)

    to = lax.broadcasted_iota(jnp.int32, (1, 512), 1)
    source = ((to >> 5) & 3) * 128 + (to >> 7) * 32 + (to & 31)
    swap = (lax.broadcasted_iota(jnp.int32, (512, 512), 0) == source).astype(jnp.float32).astype(jnp.bfloat16)

    for x in range(4):
        tiles = []
        for y in range(4):
            for zq in range(4):
                rows = [pl.ds(pl.multiple_of(starts[4 * zq + i] + x * 64 + y * 16, 16), 16) for i in range(4)]
                tiles.append(jnp.concatenate([got_ref[row, :] for row in rows], axis=1))
        moved = jnp.dot(jnp.concatenate(tiles, axis=0), swap, preferred_element_type=jnp.float32)
        for y in range(4):
            for zq in range(4):
                at = (y * 4 + zq) * 16
                lanes = slice(x * 512 + zq * 128, x * 512 + zq * 128 + 128)
                for c in range(2):
                    part = moved[at + 8 * c : at + 8 * c + 8]
                    for t in range(2):
                        early, late = part[:, t * 128 : t * 128 + 128], part[:, 256 + t * 128 : 384 + t * 128]
                        to_row = ((2 * y + c) * 2 + t) * 16
                        columns[to_row : to_row + 16, lanes] = jnp.concatenate([early, late], axis=0).astype(jnp.bfloat16)

    copy.wait()
    for n in range(4):
        total = jnp.dot(columns[...], weights[:, n * 256 : (n + 1) * 256], preferred_element_type=jnp.float32)
        peak = total[0:16]
        for t in range(1, 16):
            peak = jnp.maximum(peak, total[t * 16 : (t + 1) * 16])
        logs[:, n * 256 : (n + 1) * 256] = jnp.log(jnp.maximum(peak, 0.1))

    row = lax.broadcasted_iota(jnp.int32, (16, 128), 0)
    mine = lane == me_ref[0] * 16 + row
    base = jnp.sum(jnp.where(mine, base_ref[...].astype(jnp.float32), 0.0), axis=1, keepdims=True)
    wet = wet_ref[...].astype(jnp.float32)
    bottom = jnp.log(jnp.full((16, 1), 0.1, jnp.float32))

    @pl.loop(0, NB)
    def _(j):
        log_level = jnp.broadcast_to(bottom + 0.15 * (base + j.astype(jnp.float32)), (16, 128))
        total = jnp.zeros((16, 128), jnp.float32)
        for b in range(8):
            part = slice(b * 128, b * 128 + 128)
            total += rates_ref[:, part] * erfc((log_level - logs[:, part]) * scale)
        sums[pl.ds(pl.multiple_of(j * 16, 16), 16), :] = total

    for j in range(NB):
        hazard = jnp.sum(sums[j * 16 : j * 16 + 16, :], axis=1, keepdims=True) * (0.5 / K)
        out_ref[j : j + 1, :] = jnp.sum(jnp.where(mine, hazard, 0.0), axis=0, keepdims=True) * wet


def hazard_of(me, got, weights, rates, base, wet):
    vmem = pl.BlockSpec(memory_space=pltpu.VMEM)
    return pl.pallas_call(
        hazard_kernel,
        out_shape=jax.ShapeDtypeStruct((16, 128), jnp.float32),
        in_specs=[pl.BlockSpec(memory_space=pltpu.SMEM), vmem, pl.BlockSpec(memory_space=pl.ANY), vmem, vmem, vmem],
        out_specs=vmem,
        scratch_shapes=[
            pltpu.VMEM((256, 2048), jnp.bfloat16),
            pltpu.VMEM((2048, K), jnp.bfloat16),
            pltpu.VMEM((16, 1024), jnp.float32),
            pltpu.VMEM((256, 128), jnp.float32),
            pltpu.SemaphoreType.DMA,
        ],
        compiler_params=pltpu.CompilerParams(vmem_limit_bytes=52 * MIB),
        name="hazard_levels",
    )(me, got, weights, rates, base, wet)


def body(waveforms, scen_weights, rates, tile_cells, level_base, wet_mask):
    me, z = lax.axis_index(("y", "c")), lax.axis_index("z")

    def fetch(steps):
        ring = [(((i + steps[r]) % 16) * 8 + r, i * 8 + r) for i in range(16) for r in range(8)]
        return lax.ppermute(scen_weights.T, ("z", "y", "c"), ring)

    near, far = fetch(NEAR), fetch(FAR)
    near, far, sent = lax.optimization_barrier((near, far, gather(tile_cells, waveforms.reshape(64, C))))
    weights = lax.all_gather(jnp.concatenate([far, near], axis=0), ("x", "y", "c"), axis=0, tiled=True)
    got = lax.all_to_all(sent.reshape(512, 8, 128), EVERY, 0, 0, tiled=True)
    part = hazard_of(
        jnp.stack([me, z]),
        got.reshape(C // 2, 128),
        weights,
        rates.reshape(1, K),
        level_base.reshape(1, 128),
        wet_mask.reshape(1, 128),
    )
    hazard = lax.all_to_all(part.reshape(8, 2, 128), ("y", "c"), 0, 0, tiled=True)
    return jnp.sum(hazard, axis=0)


def solution(mesh):
    split = Mesh(mesh.devices.reshape(16, 4, 4, 2), EVERY)
    src, tm = ("z", "x"), ("y", "c")
    return jax.shard_map(
        body,
        mesh=split,
        in_specs=(P(tm, src, None), P(None, src), P(), P(), P(src), P(src)),
        out_specs=P(tm, src),
        check_vma=False,
    )
```

```python
import functools

import jax
import jax.numpy as jnp
from jax import lax
from jax.experimental import pallas as pl
from jax.experimental.pallas import tpu as pltpu
from jax.sharding import Mesh, PartitionSpec as P

K = 1024
NB = 16
C = 8192
EVERY = ("z", "x", "y", "c")
MIB = 1 << 20
NEAR = (0, 1, 15, 2, 14, 3, 13, 4)
FAR = (8, 7, 9, 6, 10, 5, 11, 12)

ERFC = (
    0.17087277,
    -0.82215223,
    1.48851587,
    -1.13520398,
    0.27886807,
    -0.18628806,
    0.09678418,
    0.37409196,
    1.00002368,
    -1.26551223,
)


def erfc(x):
    size = jnp.abs(x)
    t = 1.0 / (1.0 + 0.5 * size)
    total = jnp.full_like(t, ERFC[0])
    for c in ERFC[1:]:
        total = total * t + c
    tail = t * jnp.exp(total - x * x)
    return jnp.where(x < 0.0, 2.0 - tail, tail)


def gather_kernel(cells_hbm, wave_hbm, out_hbm, cells, wave, turned, picked, out, cells_sem, wave_sem, out_sem):
    half, part = C // 2, C // 8
    cells_copy = pltpu.make_async_copy(cells_hbm, cells, cells_sem)
    loads = []
    for k in range(4):
        for h in range(2):
            lanes = slice(h * half + k * part, h * half + (k + 1) * part)
            loads.append(pltpu.make_async_copy(wave_hbm.at[:, lanes], wave.at[:, lanes], wave_sem.at[2 * k + h]))
    for copy in loads[:2] + [cells_copy] + loads[2:]:
        copy.start()

    for k in range(4):
        loads[2 * k].wait()
        loads[2 * k + 1].wait()

        @pl.loop(k * part // 128, (k + 1) * part // 128)
        def _(j):
            low = wave[:, pl.ds(pl.multiple_of(j * 128, 128), 128)]
            high = wave[:, pl.ds(pl.multiple_of(half + j * 128, 128), 128)]
            one = jnp.concatenate([low, high], axis=0).T.astype(jnp.float32)
            two = jnp.concatenate([high, low], axis=0).T.astype(jnp.float32)
            turned[pl.ds(pl.multiple_of(j * 128, 128), 128), :] = one
            turned[pl.ds(pl.multiple_of(half + j * 128, 128), 128), :] = two
            turned[pl.ds(pl.multiple_of(C + j * 128, 128), 128), :] = one

    cells_copy.wait()
    first = lax.broadcasted_iota(jnp.int32, (1, 128), 1) < 64
    stores = []
    for k in range(4):

        @pl.loop(k * C // 256, (k + 1) * C // 256)
        def _(four):
            for e in range(4):
                for a in range(8):
                    at = four * 64 + e * 16 + a
                    one = turned[pl.ds(cells[at], 1), :]
                    two = turned[pl.ds(cells[at + 8] + half, 1), :]
                    picked[pl.ds(four * 32 + e * 8 + a, 1), :] = jnp.where(first, one, two)

        @pl.loop(k * part // 128, (k + 1) * part // 128)
        def _(i):
            rows = pl.ds(pl.multiple_of(i * 128, 128), 128)
            out[rows, :] = picked[rows, :].astype(jnp.bfloat16)

        rows = slice(k * part, (k + 1) * part)
        stores.append(pltpu.make_async_copy(out.at[rows], out_hbm.at[rows], out_sem.at[k]))
        stores[k].start()
    for copy in stores:
        copy.wait()


def gather(cells, wave):
    hbm = pl.BlockSpec(memory_space=pl.ANY)
    return pl.pallas_call(
        gather_kernel,
        out_shape=jax.ShapeDtypeStruct((C // 2, 128), jnp.bfloat16),
        in_specs=[hbm, hbm],
        out_specs=hbm,
        scratch_shapes=[
            pltpu.SMEM((C,), jnp.int32),
            pltpu.VMEM((64, C), jnp.bfloat16),
            pltpu.VMEM((C + C // 2, 128), jnp.float32),
            pltpu.VMEM((C // 2, 128), jnp.float32),
            pltpu.VMEM((C // 2, 128), jnp.bfloat16),
            pltpu.SemaphoreType.DMA,
            pltpu.SemaphoreType.DMA((8,)),
            pltpu.SemaphoreType.DMA((4,)),
        ],
        compiler_params=pltpu.CompilerParams(vmem_limit_bytes=60 * MIB),
        cost_estimate=pl.CostEstimate(flops=1 << 20, bytes_accessed=40 * MIB, transcendentals=0),
        name="gather_cells",
    )(cells, wave)


def hazard_kernel(me_ref, got_ref, weights_ref, rates_ref, base_ref, wet_ref, out_ref, columns, weights, logs, sums, sem):
    copy = pltpu.make_async_copy(weights_ref, weights, sem)
    copy.start()
    scale = 1.0 / (0.5 * jnp.sqrt(jnp.float32(2.0)))
    lane = lax.broadcasted_iota(jnp.int32, (16, 128), 1)
    starts = []
    for near, far in zip(NEAR, FAR):
        for ahead in (near, far):
            starts.append(((me_ref[1] + ahead) & 15) * 256)

    to = lax.broadcasted_iota(jnp.int32, (1, 512), 1)
    source = ((to >> 5) & 3) * 128 + (to >> 7) * 32 + (to & 31)
    swap = (lax.broadcasted_iota(jnp.int32, (512, 512), 0) == source).astype(jnp.float32).astype(jnp.bfloat16)

    for x in range(4):
        tiles = []
        for y in range(4):
            for zq in range(4):
                rows = [pl.ds(pl.multiple_of(starts[4 * zq + i] + x * 64 + y * 16, 16), 16) for i in range(4)]
                tiles.append(jnp.concatenate([got_ref[row, :] for row in rows], axis=1))
        moved = jnp.dot(jnp.concatenate(tiles, axis=0), swap, preferred_element_type=jnp.float32)
        for y in range(4):
            for zq in range(4):
                at = (y * 4 + zq) * 16
                lanes = slice(x * 512 + zq * 128, x * 512 + zq * 128 + 128)
                for c in range(2):
                    part = moved[at + 8 * c : at + 8 * c + 8]
                    for t in range(2):
                        early, late = part[:, t * 128 : t * 128 + 128], part[:, 256 + t * 128 : 384 + t * 128]
                        to_row = ((2 * y + c) * 2 + t) * 16
                        columns[to_row : to_row + 16, lanes] = jnp.concatenate([early, late], axis=0).astype(jnp.bfloat16)

    copy.wait()
    for n in range(4):
        total = jnp.dot(columns[...], weights[:, n * 256 : (n + 1) * 256], preferred_element_type=jnp.float32)
        peak = total[0:16]
        for t in range(1, 16):
            peak = jnp.maximum(peak, total[t * 16 : (t + 1) * 16])
        logs[:, n * 256 : (n + 1) * 256] = jnp.log(jnp.maximum(peak, 0.1))

    row = lax.broadcasted_iota(jnp.int32, (16, 128), 0)
    mine = lane == me_ref[0] * 16 + row
    base = jnp.sum(jnp.where(mine, base_ref[...].astype(jnp.float32), 0.0), axis=1, keepdims=True)
    wet = wet_ref[...].astype(jnp.float32)
    bottom = jnp.log(jnp.full((16, 1), 0.1, jnp.float32))

    @pl.loop(0, NB)
    def _(j):
        log_level = jnp.broadcast_to(bottom + 0.15 * (base + j.astype(jnp.float32)), (16, 128))
        total = jnp.zeros((16, 128), jnp.float32)
        for b in range(8):
            part = slice(b * 128, b * 128 + 128)
            total += rates_ref[:, part] * erfc((log_level - logs[:, part]) * scale)
        sums[pl.ds(pl.multiple_of(j * 16, 16), 16), :] = total

    for j in range(NB):
        hazard = jnp.sum(sums[j * 16 : j * 16 + 16, :], axis=1, keepdims=True) * (0.5 / K)
        out_ref[j : j + 1, :] = jnp.sum(jnp.where(mine, hazard, 0.0), axis=0, keepdims=True) * wet


def hazard_of(me, got, weights, rates, base, wet):
    vmem = pl.BlockSpec(memory_space=pltpu.VMEM)
    return pl.pallas_call(
        hazard_kernel,
        out_shape=jax.ShapeDtypeStruct((16, 128), jnp.float32),
        in_specs=[pl.BlockSpec(memory_space=pltpu.SMEM), vmem, pl.BlockSpec(memory_space=pl.ANY), vmem, vmem, vmem],
        out_specs=vmem,
        scratch_shapes=[
            pltpu.VMEM((256, 2048), jnp.bfloat16),
            pltpu.VMEM((2048, K), jnp.bfloat16),
            pltpu.VMEM((16, 1024), jnp.float32),
            pltpu.VMEM((256, 128), jnp.float32),
            pltpu.SemaphoreType.DMA,
        ],
        compiler_params=pltpu.CompilerParams(vmem_limit_bytes=52 * MIB),
        name="hazard_levels",
    )(me, got, weights, rates, base, wet)


def body(waveforms, scen_weights, rates, tile_cells, level_base, wet_mask):
    me, z = lax.axis_index(("y", "c")), lax.axis_index("z")

    def fetch(steps):
        ring = [(((i + steps[r]) % 16) * 8 + r, i * 8 + r) for i in range(16) for r in range(8)]
        return lax.ppermute(scen_weights.T, ("z", "y", "c"), ring)

    far, near = fetch(FAR), fetch(NEAR)
    far, near, sent = lax.optimization_barrier((far, near, gather(tile_cells, waveforms.reshape(64, C))))
    weights = lax.all_gather(jnp.concatenate([near, far], axis=0), ("x", "y", "c"), axis=0, tiled=True)
    got = lax.all_to_all(sent.reshape(512, 8, 128), EVERY, 0, 0, tiled=True)
    part = hazard_of(
        jnp.stack([me, z]),
        got.reshape(C // 2, 128),
        weights,
        rates.reshape(1, K),
        level_base.reshape(1, 128),
        wet_mask.reshape(1, 128),
    )
    hazard = lax.all_to_all(part.reshape(8, 2, 128), ("y", "c"), 0, 0, tiled=True)
    return jnp.sum(hazard, axis=0)


def solution(mesh):
    split = Mesh(mesh.devices.reshape(16, 4, 4, 2), EVERY)
    src, tm = ("z", "x"), ("y", "c")
    return jax.shard_map(
        body,
        mesh=split,
        in_specs=(P(tm, src, None), P(None, src), P(), P(), P(src), P(src)),
        out_specs=P(tm, src),
        check_vma=False,
    )
```

```python
import functools

import jax
import jax.numpy as jnp
from jax import lax
from jax.experimental import pallas as pl
from jax.experimental.pallas import tpu as pltpu
from jax.sharding import Mesh, PartitionSpec as P

K = 1024
NB = 16
C = 8192
EVERY = ("z", "x", "y", "c")
MIB = 1 << 20
NEAR = (0, 1, 15, 2, 14, 3, 13, 4)
FAR = (8, 7, 9, 6, 10, 5, 11, 12)

ERFC = (
    0.17087277,
    -0.82215223,
    1.48851587,
    -1.13520398,
    0.27886807,
    -0.18628806,
    0.09678418,
    0.37409196,
    1.00002368,
    -1.26551223,
)


def erfc(x):
    size = jnp.abs(x)
    t = 1.0 / (1.0 + 0.5 * size)
    total = jnp.full_like(t, ERFC[0])
    for c in ERFC[1:]:
        total = total * t + c
    tail = t * jnp.exp(total - x * x)
    return jnp.where(x < 0.0, 2.0 - tail, tail)


def gather_kernel(cells_hbm, wave_hbm, out_hbm, cells, wave, turned, picked, out, cells_sem, wave_sem, out_sem):
    half, part = C // 2, C // 8
    cells_copy = pltpu.make_async_copy(cells_hbm, cells, cells_sem)
    loads = []
    for k in range(4):
        for h in range(2):
            lanes = slice(h * half + k * part, h * half + (k + 1) * part)
            loads.append(pltpu.make_async_copy(wave_hbm.at[:, lanes], wave.at[:, lanes], wave_sem.at[2 * k + h]))
    for copy in loads[:2] + [cells_copy] + loads[2:]:
        copy.start()

    for k in range(4):
        loads[2 * k].wait()
        loads[2 * k + 1].wait()

        @pl.loop(k * part // 128, (k + 1) * part // 128)
        def _(j):
            low = wave[:, pl.ds(pl.multiple_of(j * 128, 128), 128)]
            high = wave[:, pl.ds(pl.multiple_of(half + j * 128, 128), 128)]
            one = jnp.concatenate([low, high], axis=0).T.astype(jnp.float32)
            two = jnp.concatenate([high, low], axis=0).T.astype(jnp.float32)
            turned[pl.ds(pl.multiple_of(j * 128, 128), 128), :] = one
            turned[pl.ds(pl.multiple_of(half + j * 128, 128), 128), :] = two
            turned[pl.ds(pl.multiple_of(C + j * 128, 128), 128), :] = one

    cells_copy.wait()
    first = lax.broadcasted_iota(jnp.int32, (1, 128), 1) < 64
    stores = []
    for k in range(4):

        @pl.loop(k * C // 256, (k + 1) * C // 256)
        def _(four):
            for e in range(4):
                for a in range(8):
                    at = four * 64 + e * 16 + a
                    one = turned[pl.ds(cells[at], 1), :]
                    two = turned[pl.ds(cells[at + 8] + half, 1), :]
                    picked[pl.ds(four * 32 + e * 8 + a, 1), :] = jnp.where(first, one, two)

        @pl.loop(k * part // 128, (k + 1) * part // 128)
        def _(i):
            rows = pl.ds(pl.multiple_of(i * 128, 128), 128)
            out[rows, :] = picked[rows, :].astype(jnp.bfloat16)

        rows = slice(k * part, (k + 1) * part)
        stores.append(pltpu.make_async_copy(out.at[rows], out_hbm.at[rows], out_sem.at[k]))
        stores[k].start()
    for copy in stores:
        copy.wait()


def gather(cells, wave):
    hbm = pl.BlockSpec(memory_space=pl.ANY)
    return pl.pallas_call(
        gather_kernel,
        out_shape=jax.ShapeDtypeStruct((C // 2, 128), jnp.bfloat16),
        in_specs=[hbm, hbm],
        out_specs=hbm,
        scratch_shapes=[
            pltpu.SMEM((C,), jnp.int32),
            pltpu.VMEM((64, C), jnp.bfloat16),
            pltpu.VMEM((C + C // 2, 128), jnp.float32),
            pltpu.VMEM((C // 2, 128), jnp.float32),
            pltpu.VMEM((C // 2, 128), jnp.bfloat16),
            pltpu.SemaphoreType.DMA,
            pltpu.SemaphoreType.DMA((8,)),
            pltpu.SemaphoreType.DMA((4,)),
        ],
        compiler_params=pltpu.CompilerParams(vmem_limit_bytes=60 * MIB),
        cost_estimate=pl.CostEstimate(flops=1 << 20, bytes_accessed=40 * MIB, transcendentals=0),
        name="gather_cells",
    )(cells, wave)


def hazard_kernel(me_ref, got_ref, weights_ref, rates_ref, base_ref, wet_ref, out_ref, columns, weights, logs, sums, sem):
    copy = pltpu.make_async_copy(weights_ref, weights, sem)
    copy.start()
    scale = 1.0 / (0.5 * jnp.sqrt(jnp.float32(2.0)))
    lane = lax.broadcasted_iota(jnp.int32, (16, 128), 1)
    starts = []
    for near, far in zip(NEAR, FAR):
        for ahead in (far, near):
            starts.append(((me_ref[1] + ahead) & 15) * 256)

    to = lax.broadcasted_iota(jnp.int32, (1, 512), 1)
    source = ((to >> 5) & 3) * 128 + (to >> 7) * 32 + (to & 31)
    swap = (lax.broadcasted_iota(jnp.int32, (512, 512), 0) == source).astype(jnp.float32).astype(jnp.bfloat16)

    for x in range(4):
        tiles = []
        for y in range(4):
            for zq in range(4):
                rows = [pl.ds(pl.multiple_of(starts[4 * zq + i] + x * 64 + y * 16, 16), 16) for i in range(4)]
                tiles.append(jnp.concatenate([got_ref[row, :] for row in rows], axis=1))
        moved = jnp.dot(jnp.concatenate(tiles, axis=0), swap, preferred_element_type=jnp.float32)
        for y in range(4):
            for zq in range(4):
                at = (y * 4 + zq) * 16
                lanes = slice(x * 512 + zq * 128, x * 512 + zq * 128 + 128)
                for c in range(2):
                    part = moved[at + 8 * c : at + 8 * c + 8]
                    for t in range(2):
                        early, late = part[:, t * 128 : t * 128 + 128], part[:, 256 + t * 128 : 384 + t * 128]
                        to_row = ((2 * y + c) * 2 + t) * 16
                        columns[to_row : to_row + 16, lanes] = jnp.concatenate([early, late], axis=0).astype(jnp.bfloat16)

    copy.wait()
    for n in range(4):
        total = jnp.dot(columns[...], weights[:, n * 256 : (n + 1) * 256], preferred_element_type=jnp.float32)
        peak = total[0:16]
        for t in range(1, 16):
            peak = jnp.maximum(peak, total[t * 16 : (t + 1) * 16])
        logs[:, n * 256 : (n + 1) * 256] = jnp.log(jnp.maximum(peak, 0.1))

    row = lax.broadcasted_iota(jnp.int32, (16, 128), 0)
    mine = lane == me_ref[0] * 16 + row
    base = jnp.sum(jnp.where(mine, base_ref[...].astype(jnp.float32), 0.0), axis=1, keepdims=True)
    wet = wet_ref[...].astype(jnp.float32)
    bottom = jnp.log(jnp.full((16, 1), 0.1, jnp.float32))

    @pl.loop(0, NB)
    def _(j):
        log_level = jnp.broadcast_to(bottom + 0.15 * (base + j.astype(jnp.float32)), (16, 128))
        total = jnp.zeros((16, 128), jnp.float32)
        for b in range(8):
            part = slice(b * 128, b * 128 + 128)
            total += rates_ref[:, part] * erfc((log_level - logs[:, part]) * scale)
        sums[pl.ds(pl.multiple_of(j * 16, 16), 16), :] = total

    for j in range(NB):
        hazard = jnp.sum(sums[j * 16 : j * 16 + 16, :], axis=1, keepdims=True) * (0.5 / K)
        out_ref[j : j + 1, :] = jnp.sum(jnp.where(mine, hazard, 0.0), axis=0, keepdims=True) * wet


def hazard_of(me, got, weights, rates, base, wet):
    vmem = pl.BlockSpec(memory_space=pltpu.VMEM)
    return pl.pallas_call(
        hazard_kernel,
        out_shape=jax.ShapeDtypeStruct((16, 128), jnp.float32),
        in_specs=[pl.BlockSpec(memory_space=pltpu.SMEM), vmem, pl.BlockSpec(memory_space=pl.ANY), vmem, vmem, vmem],
        out_specs=vmem,
        scratch_shapes=[
            pltpu.VMEM((256, 2048), jnp.bfloat16),
            pltpu.VMEM((2048, K), jnp.bfloat16),
            pltpu.VMEM((16, 1024), jnp.float32),
            pltpu.VMEM((256, 128), jnp.float32),
            pltpu.SemaphoreType.DMA,
        ],
        compiler_params=pltpu.CompilerParams(vmem_limit_bytes=52 * MIB),
        name="hazard_levels",
    )(me, got, weights, rates, base, wet)


def body(waveforms, scen_weights, rates, tile_cells, level_base, wet_mask):
    me, z = lax.axis_index(("y", "c")), lax.axis_index("z")

    def fetch(steps):
        ring = [(((i + steps[r]) % 16) * 8 + r, i * 8 + r) for i in range(16) for r in range(8)]
        return lax.ppermute(scen_weights.T, ("z", "y", "c"), ring)

    near, far = fetch(NEAR), fetch(FAR)
    near, far, sent = lax.optimization_barrier((near, far, gather(tile_cells, waveforms.reshape(64, C))))
    weights = lax.all_gather(jnp.concatenate([far, near], axis=0), ("x", "y", "c"), axis=0, tiled=True)
    got = lax.all_to_all(sent.reshape(512, 8, 128), EVERY, 0, 0, tiled=True)
    part = hazard_of(
        jnp.stack([me, z]),
        got.reshape(C // 2, 128),
        weights,
        rates.reshape(1, K),
        level_base.reshape(1, 128),
        wet_mask.reshape(1, 128),
    )
    hazard = lax.all_to_all(part.reshape(8, 2, 128), ("y", "c"), 0, 0, tiled=True)
    return jnp.sum(hazard, axis=0)


def solution(mesh):
    split = Mesh(mesh.devices.reshape(16, 4, 4, 2), EVERY)
    src, tm = ("z", "x"), ("y", "c")
    return jax.shard_map(
        body,
        mesh=split,
        in_specs=(P(tm, src, None), P(None, src), P(), P(), P(src), P(src)),
        out_specs=P(tm, src),
        check_vma=False,
    )
```

```python
import functools

import jax
import jax.numpy as jnp
from jax import lax
from jax.experimental import pallas as pl
from jax.experimental.pallas import tpu as pltpu
from jax.sharding import Mesh, PartitionSpec as P

K = 1024
NB = 16
C = 8192
EVERY = ("z", "x", "y", "c")
MIB = 1 << 20
NEAR = (0, 1, 15, 2, 14, 3, 13, 4)
FAR = (8, 9, 7, 10, 6, 11, 5, 12)

ERFC = (
    0.17087277,
    -0.82215223,
    1.48851587,
    -1.13520398,
    0.27886807,
    -0.18628806,
    0.09678418,
    0.37409196,
    1.00002368,
    -1.26551223,
)


def erfc(x):
    size = jnp.abs(x)
    t = 1.0 / (1.0 + 0.5 * size)
    total = jnp.full_like(t, ERFC[0])
    for c in ERFC[1:]:
        total = total * t + c
    tail = t * jnp.exp(total - x * x)
    return jnp.where(x < 0.0, 2.0 - tail, tail)


def gather_kernel(cells_hbm, wave_hbm, out_hbm, cells, wave, turned, picked, out, cells_sem, wave_sem, out_sem):
    half, part = C // 2, C // 8
    cells_copy = pltpu.make_async_copy(cells_hbm, cells, cells_sem)
    loads = []
    for k in range(4):
        for h in range(2):
            lanes = slice(h * half + k * part, h * half + (k + 1) * part)
            loads.append(pltpu.make_async_copy(wave_hbm.at[:, lanes], wave.at[:, lanes], wave_sem.at[2 * k + h]))
    for copy in loads[:2] + [cells_copy] + loads[2:]:
        copy.start()

    for k in range(4):
        loads[2 * k].wait()
        loads[2 * k + 1].wait()

        @pl.loop(k * part // 128, (k + 1) * part // 128)
        def _(j):
            low = wave[:, pl.ds(pl.multiple_of(j * 128, 128), 128)]
            high = wave[:, pl.ds(pl.multiple_of(half + j * 128, 128), 128)]
            one = jnp.concatenate([low, high], axis=0).T.astype(jnp.float32)
            two = jnp.concatenate([high, low], axis=0).T.astype(jnp.float32)
            turned[pl.ds(pl.multiple_of(j * 128, 128), 128), :] = one
            turned[pl.ds(pl.multiple_of(half + j * 128, 128), 128), :] = two
            turned[pl.ds(pl.multiple_of(C + j * 128, 128), 128), :] = one

    cells_copy.wait()
    first = lax.broadcasted_iota(jnp.int32, (1, 128), 1) < 64
    stores = []
    for k in range(4):

        @pl.loop(k * C // 256, (k + 1) * C // 256)
        def _(four):
            for e in range(4):
                for a in range(8):
                    at = four * 64 + e * 16 + a
                    one = turned[pl.ds(cells[at], 1), :]
                    two = turned[pl.ds(cells[at + 8] + half, 1), :]
                    picked[pl.ds(four * 32 + e * 8 + a, 1), :] = jnp.where(first, one, two)

        @pl.loop(k * part // 128, (k + 1) * part // 128)
        def _(i):
            rows = pl.ds(pl.multiple_of(i * 128, 128), 128)
            out[rows, :] = picked[rows, :].astype(jnp.bfloat16)

        rows = slice(k * part, (k + 1) * part)
        stores.append(pltpu.make_async_copy(out.at[rows], out_hbm.at[rows], out_sem.at[k]))
        stores[k].start()
    for copy in stores:
        copy.wait()


def gather(cells, wave):
    hbm = pl.BlockSpec(memory_space=pl.ANY)
    return pl.pallas_call(
        gather_kernel,
        out_shape=jax.ShapeDtypeStruct((C // 2, 128), jnp.bfloat16),
        in_specs=[hbm, hbm],
        out_specs=hbm,
        scratch_shapes=[
            pltpu.SMEM((C,), jnp.int32),
            pltpu.VMEM((64, C), jnp.bfloat16),
            pltpu.VMEM((C + C // 2, 128), jnp.float32),
            pltpu.VMEM((C // 2, 128), jnp.float32),
            pltpu.VMEM((C // 2, 128), jnp.bfloat16),
            pltpu.SemaphoreType.DMA,
            pltpu.SemaphoreType.DMA((8,)),
            pltpu.SemaphoreType.DMA((4,)),
        ],
        compiler_params=pltpu.CompilerParams(vmem_limit_bytes=60 * MIB),
        cost_estimate=pl.CostEstimate(flops=1 << 20, bytes_accessed=40 * MIB, transcendentals=0),
        name="gather_cells",
    )(cells, wave)


def hazard_kernel(me_ref, got_ref, weights_ref, rates_ref, base_ref, wet_ref, out_ref, columns, weights, logs, sums, sem):
    copy = pltpu.make_async_copy(weights_ref, weights, sem)
    copy.start()
    scale = 1.0 / (0.5 * jnp.sqrt(jnp.float32(2.0)))
    lane = lax.broadcasted_iota(jnp.int32, (16, 128), 1)
    starts = []
    for near, far in zip(NEAR, FAR):
        for ahead in (near, far):
            starts.append(((me_ref[1] + ahead) & 15) * 256)

    to = lax.broadcasted_iota(jnp.int32, (1, 512), 1)
    source = ((to >> 5) & 3) * 128 + (to >> 7) * 32 + (to & 31)
    swap = (lax.broadcasted_iota(jnp.int32, (512, 512), 0) == source).astype(jnp.float32).astype(jnp.bfloat16)

    for x in range(4):
        tiles = []
        for y in range(4):
            for zq in range(4):
                rows = [pl.ds(pl.multiple_of(starts[4 * zq + i] + x * 64 + y * 16, 16), 16) for i in range(4)]
                tiles.append(jnp.concatenate([got_ref[row, :] for row in rows], axis=1))
        moved = jnp.dot(jnp.concatenate(tiles, axis=0), swap, preferred_element_type=jnp.float32)
        for y in range(4):
            for zq in range(4):
                at = (y * 4 + zq) * 16
                lanes = slice(x * 512 + zq * 128, x * 512 + zq * 128 + 128)
                for c in range(2):
                    part = moved[at + 8 * c : at + 8 * c + 8]
                    for t in range(2):
                        early, late = part[:, t * 128 : t * 128 + 128], part[:, 256 + t * 128 : 384 + t * 128]
                        to_row = ((2 * y + c) * 2 + t) * 16
                        columns[to_row : to_row + 16, lanes] = jnp.concatenate([early, late], axis=0).astype(jnp.bfloat16)

    copy.wait()
    for n in range(4):
        total = jnp.dot(columns[...], weights[:, n * 256 : (n + 1) * 256], preferred_element_type=jnp.float32)
        peak = total[0:16]
        for t in range(1, 16):
            peak = jnp.maximum(peak, total[t * 16 : (t + 1) * 16])
        logs[:, n * 256 : (n + 1) * 256] = jnp.log(jnp.maximum(peak, 0.1))

    row = lax.broadcasted_iota(jnp.int32, (16, 128), 0)
    mine = lane == me_ref[0] * 16 + row
    base = jnp.sum(jnp.where(mine, base_ref[...].astype(jnp.float32), 0.0), axis=1, keepdims=True)
    wet = wet_ref[...].astype(jnp.float32)
    bottom = jnp.log(jnp.full((16, 1), 0.1, jnp.float32))

    @pl.loop(0, NB, unroll=4)
    def _(j):
        log_level = jnp.broadcast_to(bottom + 0.15 * (base + j.astype(jnp.float32)), (16, 128))
        total = jnp.zeros((16, 128), jnp.float32)
        for b in range(8):
            part = slice(b * 128, b * 128 + 128)
            total += rates_ref[:, part] * erfc((log_level - logs[:, part]) * scale)
        sums[pl.ds(pl.multiple_of(j * 16, 16), 16), :] = total

    for j in range(NB):
        hazard = jnp.sum(sums[j * 16 : j * 16 + 16, :], axis=1, keepdims=True) * (0.5 / K)
        out_ref[j : j + 1, :] = jnp.sum(jnp.where(mine, hazard, 0.0), axis=0, keepdims=True) * wet


def hazard_of(me, got, weights, rates, base, wet):
    vmem = pl.BlockSpec(memory_space=pltpu.VMEM)
    return pl.pallas_call(
        hazard_kernel,
        out_shape=jax.ShapeDtypeStruct((16, 128), jnp.float32),
        in_specs=[pl.BlockSpec(memory_space=pltpu.SMEM), vmem, pl.BlockSpec(memory_space=pl.ANY), vmem, vmem, vmem],
        out_specs=vmem,
        scratch_shapes=[
            pltpu.VMEM((256, 2048), jnp.bfloat16),
            pltpu.VMEM((2048, K), jnp.bfloat16),
            pltpu.VMEM((16, 1024), jnp.float32),
            pltpu.VMEM((256, 128), jnp.float32),
            pltpu.SemaphoreType.DMA,
        ],
        compiler_params=pltpu.CompilerParams(vmem_limit_bytes=52 * MIB),
        name="hazard_levels",
    )(me, got, weights, rates, base, wet)


def body(waveforms, scen_weights, rates, tile_cells, level_base, wet_mask):
    me, z = lax.axis_index(("y", "c")), lax.axis_index("z")

    def fetch(steps):
        ring = [(((i + steps[r]) % 16) * 8 + r, i * 8 + r) for i in range(16) for r in range(8)]
        return lax.ppermute(scen_weights.T, ("z", "y", "c"), ring)

    far, near = fetch(FAR), fetch(NEAR)
    far, near, sent = lax.optimization_barrier((far, near, gather(tile_cells, waveforms.reshape(64, C))))
    weights = lax.all_gather(jnp.concatenate([near, far], axis=0), ("x", "y", "c"), axis=0, tiled=True)
    got = lax.all_to_all(sent.reshape(512, 8, 128), EVERY, 0, 0, tiled=True)
    part = hazard_of(
        jnp.stack([me, z]),
        got.reshape(C // 2, 128),
        weights,
        rates.reshape(1, K),
        level_base.reshape(1, 128),
        wet_mask.reshape(1, 128),
    )
    hazard = lax.all_to_all(part.reshape(8, 2, 128), ("y", "c"), 0, 0, tiled=True)
    return jnp.sum(hazard, axis=0)


def solution(mesh):
    split = Mesh(mesh.devices.reshape(16, 4, 4, 2), EVERY)
    src, tm = ("z", "x"), ("y", "c")
    return jax.shard_map(
        body,
        mesh=split,
        in_specs=(P(tm, src, None), P(None, src), P(), P(), P(src), P(src)),
        out_specs=P(tm, src),
        check_vma=False,
    )
```

```python
import functools

import jax
import jax.numpy as jnp
from jax import lax
from jax.experimental import pallas as pl
from jax.experimental.pallas import tpu as pltpu
from jax.sharding import Mesh, PartitionSpec as P

K = 1024
NB = 16
C = 8192
EVERY = ("z", "x", "y", "c")
MIB = 1 << 20
NEAR = (0, 1, 15, 2, 14, 3, 13, 4)
FAR = (8, 7, 9, 6, 10, 5, 11, 12)

ERFC = (
    0.17087277,
    -0.82215223,
    1.48851587,
    -1.13520398,
    0.27886807,
    -0.18628806,
    0.09678418,
    0.37409196,
    1.00002368,
    -1.26551223,
)


def erfc(x):
    size = jnp.abs(x)
    t = 1.0 / (1.0 + 0.5 * size)
    total = jnp.full_like(t, ERFC[0])
    for c in ERFC[1:]:
        total = total * t + c
    tail = t * jnp.exp(total - x * x)
    return jnp.where(x < 0.0, 2.0 - tail, tail)


def gather_kernel(cells_hbm, wave_hbm, out_hbm, cells, wave, turned, picked, out, cells_sem, wave_sem, out_sem):
    half, part = C // 2, C // 8
    cells_copy = pltpu.make_async_copy(cells_hbm, cells, cells_sem)
    loads = []
    for k in range(4):
        for h in range(2):
            lanes = slice(h * half + k * part, h * half + (k + 1) * part)
            loads.append(pltpu.make_async_copy(wave_hbm.at[:, lanes], wave.at[:, lanes], wave_sem.at[2 * k + h]))
    for copy in loads[:2] + [cells_copy] + loads[2:]:
        copy.start()

    for k in range(4):
        loads[2 * k].wait()
        loads[2 * k + 1].wait()

        @pl.loop(k * part // 128, (k + 1) * part // 128)
        def _(j):
            low = wave[:, pl.ds(pl.multiple_of(j * 128, 128), 128)]
            high = wave[:, pl.ds(pl.multiple_of(half + j * 128, 128), 128)]
            one = jnp.concatenate([low, high], axis=0).T.astype(jnp.float32)
            two = jnp.concatenate([high, low], axis=0).T.astype(jnp.float32)
            turned[pl.ds(pl.multiple_of(j * 128, 128), 128), :] = one
            turned[pl.ds(pl.multiple_of(half + j * 128, 128), 128), :] = two
            turned[pl.ds(pl.multiple_of(C + j * 128, 128), 128), :] = one

    cells_copy.wait()
    first = lax.broadcasted_iota(jnp.int32, (1, 128), 1) < 64
    stores = []
    for k in range(4):

        @pl.loop(k * C // 256, (k + 1) * C // 256)
        def _(four):
            for e in range(4):
                for a in range(8):
                    at = four * 64 + e * 16 + a
                    one = turned[pl.ds(cells[at], 1), :]
                    two = turned[pl.ds(cells[at + 8] + half, 1), :]
                    picked[pl.ds(four * 32 + e * 8 + a, 1), :] = jnp.where(first, one, two)

        @pl.loop(k * part // 128, (k + 1) * part // 128)
        def _(i):
            rows = pl.ds(pl.multiple_of(i * 128, 128), 128)
            out[rows, :] = picked[rows, :].astype(jnp.bfloat16)

        rows = slice(k * part, (k + 1) * part)
        stores.append(pltpu.make_async_copy(out.at[rows], out_hbm.at[rows], out_sem.at[k]))
        stores[k].start()
    for copy in stores:
        copy.wait()


def gather(cells, wave):
    hbm = pl.BlockSpec(memory_space=pl.ANY)
    return pl.pallas_call(
        gather_kernel,
        out_shape=jax.ShapeDtypeStruct((C // 2, 128), jnp.bfloat16),
        in_specs=[hbm, hbm],
        out_specs=hbm,
        scratch_shapes=[
            pltpu.SMEM((C,), jnp.int32),
            pltpu.VMEM((64, C), jnp.bfloat16),
            pltpu.VMEM((C + C // 2, 128), jnp.float32),
            pltpu.VMEM((C // 2, 128), jnp.float32),
            pltpu.VMEM((C // 2, 128), jnp.bfloat16),
            pltpu.SemaphoreType.DMA,
            pltpu.SemaphoreType.DMA((8,)),
            pltpu.SemaphoreType.DMA((4,)),
        ],
        compiler_params=pltpu.CompilerParams(vmem_limit_bytes=60 * MIB),
        cost_estimate=pl.CostEstimate(flops=1 << 20, bytes_accessed=40 * MIB, transcendentals=0),
        name="gather_cells",
    )(cells, wave)


def hazard_kernel(me_ref, got_ref, weights_ref, rates_ref, base_ref, wet_ref, out_ref, columns, weights, logs, sums, sem):
    copy = pltpu.make_async_copy(weights_ref, weights, sem)
    copy.start()
    scale = 1.0 / (0.5 * jnp.sqrt(jnp.float32(2.0)))
    lane = lax.broadcasted_iota(jnp.int32, (16, 128), 1)
    starts = []
    for near, far in zip(NEAR, FAR):
        for ahead in (near, far):
            starts.append(((me_ref[1] + ahead) & 15) * 256)

    to = lax.broadcasted_iota(jnp.int32, (1, 512), 1)
    source = ((to >> 5) & 3) * 128 + (to >> 7) * 32 + (to & 31)
    swap = (lax.broadcasted_iota(jnp.int32, (512, 512), 0) == source).astype(jnp.float32).astype(jnp.bfloat16)

    for x in range(4):
        tiles = []
        for y in range(4):
            for zq in range(4):
                rows = [pl.ds(pl.multiple_of(starts[4 * zq + i] + x * 64 + y * 16, 16), 16) for i in range(4)]
                tiles.append(jnp.concatenate([got_ref[row, :] for row in rows], axis=1))
        moved = jnp.dot(jnp.concatenate(tiles, axis=0), swap, preferred_element_type=jnp.float32)
        for y in range(4):
            for zq in range(4):
                at = (y * 4 + zq) * 16
                lanes = slice(x * 512 + zq * 128, x * 512 + zq * 128 + 128)
                for c in range(2):
                    part = moved[at + 8 * c : at + 8 * c + 8]
                    for t in range(2):
                        early, late = part[:, t * 128 : t * 128 + 128], part[:, 256 + t * 128 : 384 + t * 128]
                        to_row = ((2 * y + c) * 2 + t) * 16
                        columns[to_row : to_row + 16, lanes] = jnp.concatenate([early, late], axis=0).astype(jnp.bfloat16)

    copy.wait()
    for n in range(4):
        total = jnp.dot(columns[...], weights[:, n * 256 : (n + 1) * 256], preferred_element_type=jnp.float32)
        peak = total[0:16]
        for t in range(1, 16):
            peak = jnp.maximum(peak, total[t * 16 : (t + 1) * 16])
        logs[:, n * 256 : (n + 1) * 256] = jnp.log(jnp.maximum(peak, 0.1))

    row = lax.broadcasted_iota(jnp.int32, (16, 128), 0)
    mine = lane == me_ref[0] * 16 + row
    base = jnp.sum(jnp.where(mine, base_ref[...].astype(jnp.float32), 0.0), axis=1, keepdims=True)
    wet = wet_ref[...].astype(jnp.float32)
    bottom = jnp.log(jnp.full((16, 1), 0.1, jnp.float32))

    @pl.loop(0, NB, unroll=4)
    def _(j):
        log_level = jnp.broadcast_to(bottom + 0.15 * (base + j.astype(jnp.float32)), (16, 128))
        total = jnp.zeros((16, 128), jnp.float32)
        for b in range(8):
            part = slice(b * 128, b * 128 + 128)
            total += rates_ref[:, part] * erfc((log_level - logs[:, part]) * scale)
        sums[pl.ds(pl.multiple_of(j * 16, 16), 16), :] = total

    for j in range(NB):
        hazard = jnp.sum(sums[j * 16 : j * 16 + 16, :], axis=1, keepdims=True) * (0.5 / K)
        out_ref[j : j + 1, :] = jnp.sum(jnp.where(mine, hazard, 0.0), axis=0, keepdims=True) * wet


def hazard_of(me, got, weights, rates, base, wet):
    vmem = pl.BlockSpec(memory_space=pltpu.VMEM)
    return pl.pallas_call(
        hazard_kernel,
        out_shape=jax.ShapeDtypeStruct((16, 128), jnp.float32),
        in_specs=[pl.BlockSpec(memory_space=pltpu.SMEM), vmem, pl.BlockSpec(memory_space=pl.ANY), vmem, vmem, vmem],
        out_specs=vmem,
        scratch_shapes=[
            pltpu.VMEM((256, 2048), jnp.bfloat16),
            pltpu.VMEM((2048, K), jnp.bfloat16),
            pltpu.VMEM((16, 1024), jnp.float32),
            pltpu.VMEM((256, 128), jnp.float32),
            pltpu.SemaphoreType.DMA,
        ],
        compiler_params=pltpu.CompilerParams(vmem_limit_bytes=52 * MIB),
        name="hazard_levels",
    )(me, got, weights, rates, base, wet)


def body(waveforms, scen_weights, rates, tile_cells, level_base, wet_mask):
    me, z = lax.axis_index(("y", "c")), lax.axis_index("z")

    def fetch(steps):
        ring = [(((i + steps[r]) % 16) * 8 + r, i * 8 + r) for i in range(16) for r in range(8)]
        return lax.ppermute(scen_weights.T, ("z", "y", "c"), ring)

    far, near = fetch(FAR), fetch(NEAR)
    far, near, sent = lax.optimization_barrier((far, near, gather(tile_cells, waveforms.reshape(64, C))))
    weights = lax.all_gather(jnp.concatenate([near, far], axis=0), ("x", "y", "c"), axis=0, tiled=True)
    got = lax.all_to_all(sent.reshape(512, 8, 128), EVERY, 0, 0, tiled=True)
    part = hazard_of(
        jnp.stack([me, z]),
        got.reshape(C // 2, 128),
        weights,
        rates.reshape(1, K),
        level_base.reshape(1, 128),
        wet_mask.reshape(1, 128),
    )
    hazard = lax.all_to_all(part.reshape(8, 2, 128), ("y", "c"), 0, 0, tiled=True)
    return jnp.sum(hazard, axis=0)


def solution(mesh):
    split = Mesh(mesh.devices.reshape(16, 4, 4, 2), EVERY)
    src, tm = ("z", "x"), ("y", "c")
    return jax.shard_map(
        body,
        mesh=split,
        in_specs=(P(tm, src, None), P(None, src), P(), P(), P(src), P(src)),
        out_specs=P(tm, src),
        check_vma=False,
    )
```

```python
import functools

import jax
import jax.numpy as jnp
from jax import lax
from jax.experimental import pallas as pl
from jax.experimental.pallas import tpu as pltpu
from jax.sharding import Mesh, PartitionSpec as P

K = 1024
NB = 16
C = 8192
EVERY = ("z", "x", "y", "c")
MIB = 1 << 20
NEAR = (0, 1, 15, 2, 14, 3, 13, 4)
FAR = (8, 7, 9, 6, 10, 5, 11, 12)

ERFC = (
    0.17087277,
    -0.82215223,
    1.48851587,
    -1.13520398,
    0.27886807,
    -0.18628806,
    0.09678418,
    0.37409196,
    1.00002368,
    -1.26551223,
)


def erfc(x):
    size = jnp.abs(x)
    t = 1.0 / (1.0 + 0.5 * size)
    total = jnp.full_like(t, ERFC[0])
    for c in ERFC[1:]:
        total = total * t + c
    tail = t * jnp.exp(total - x * x)
    return jnp.where(x < 0.0, 2.0 - tail, tail)


def gather_kernel(cells_hbm, wave_hbm, out_hbm, cells, wave, turned, picked, out, cells_sem, wave_sem, out_sem):
    half, part = C // 2, C // 8
    cells_copy = pltpu.make_async_copy(cells_hbm, cells, cells_sem)
    loads = []
    for k in range(4):
        for h in range(2):
            lanes = slice(h * half + k * part, h * half + (k + 1) * part)
            loads.append(pltpu.make_async_copy(wave_hbm.at[:, lanes], wave.at[:, lanes], wave_sem.at[2 * k + h]))
    for copy in loads[:2] + [cells_copy] + loads[2:]:
        copy.start()

    for k in range(4):
        loads[2 * k].wait()
        loads[2 * k + 1].wait()

        @pl.loop(k * part // 128, (k + 1) * part // 128)
        def _(j):
            low = wave[:, pl.ds(pl.multiple_of(j * 128, 128), 128)]
            high = wave[:, pl.ds(pl.multiple_of(half + j * 128, 128), 128)]
            one = jnp.concatenate([low, high], axis=0).T.astype(jnp.float32)
            two = jnp.concatenate([high, low], axis=0).T.astype(jnp.float32)
            turned[pl.ds(pl.multiple_of(j * 128, 128), 128), :] = one
            turned[pl.ds(pl.multiple_of(half + j * 128, 128), 128), :] = two
            turned[pl.ds(pl.multiple_of(C + j * 128, 128), 128), :] = one

    cells_copy.wait()
    first = lax.broadcasted_iota(jnp.int32, (1, 128), 1) < 64
    stores = []
    for k in range(4):

        @pl.loop(k * C // 256, (k + 1) * C // 256)
        def _(four):
            for e in range(4):
                for a in range(8):
                    at = four * 64 + e * 16 + a
                    one = turned[pl.ds(cells[at], 1), :]
                    two = turned[pl.ds(cells[at + 8] + half, 1), :]
                    picked[pl.ds(four * 32 + e * 8 + a, 1), :] = jnp.where(first, one, two)

        @pl.loop(k * part // 128, (k + 1) * part // 128)
        def _(i):
            rows = pl.ds(pl.multiple_of(i * 128, 128), 128)
            out[rows, :] = picked[rows, :].astype(jnp.bfloat16)

        rows = slice(k * part, (k + 1) * part)
        stores.append(pltpu.make_async_copy(out.at[rows], out_hbm.at[rows], out_sem.at[k]))
        stores[k].start()
    for copy in stores:
        copy.wait()


def gather(cells, wave):
    hbm = pl.BlockSpec(memory_space=pl.ANY)
    return pl.pallas_call(
        gather_kernel,
        out_shape=jax.ShapeDtypeStruct((C // 2, 128), jnp.bfloat16),
        in_specs=[hbm, hbm],
        out_specs=hbm,
        scratch_shapes=[
            pltpu.SMEM((C,), jnp.int32),
            pltpu.VMEM((64, C), jnp.bfloat16),
            pltpu.VMEM((C + C // 2, 128), jnp.float32),
            pltpu.VMEM((C // 2, 128), jnp.float32),
            pltpu.VMEM((C // 2, 128), jnp.bfloat16),
            pltpu.SemaphoreType.DMA,
            pltpu.SemaphoreType.DMA((8,)),
            pltpu.SemaphoreType.DMA((4,)),
        ],
        compiler_params=pltpu.CompilerParams(vmem_limit_bytes=60 * MIB),
        cost_estimate=pl.CostEstimate(flops=1 << 20, bytes_accessed=40 * MIB, transcendentals=0),
        name="gather_cells",
    )(cells, wave)


def hazard_kernel(me_ref, got_ref, weights_ref, rates_ref, base_ref, wet_ref, out_ref, columns, weights, logs, sums, sem):
    copy = pltpu.make_async_copy(weights_ref, weights, sem)
    copy.start()
    scale = 1.0 / (0.5 * jnp.sqrt(jnp.float32(2.0)))
    lane = lax.broadcasted_iota(jnp.int32, (16, 128), 1)
    starts = []
    for near, far in zip(NEAR, FAR):
        for ahead in (near, far):
            starts.append(((me_ref[1] + ahead) & 15) * 256)

    to = lax.broadcasted_iota(jnp.int32, (1, 512), 1)
    source = ((to >> 5) & 3) * 128 + (to >> 7) * 32 + (to & 31)
    swap = (lax.broadcasted_iota(jnp.int32, (512, 512), 0) == source).astype(jnp.float32).astype(jnp.bfloat16)

    for x in range(4):
        tiles = []
        for y in range(4):
            for zq in range(4):
                rows = [pl.ds(pl.multiple_of(starts[4 * zq + i] + x * 64 + y * 16, 16), 16) for i in range(4)]
                tiles.append(jnp.concatenate([got_ref[row, :] for row in rows], axis=1))
        moved = jnp.dot(jnp.concatenate(tiles, axis=0), swap, preferred_element_type=jnp.float32)
        for y in range(4):
            for zq in range(4):
                at = (y * 4 + zq) * 16
                lanes = slice(x * 512 + zq * 128, x * 512 + zq * 128 + 128)
                for c in range(2):
                    part = moved[at + 8 * c : at + 8 * c + 8]
                    for t in range(2):
                        early, late = part[:, t * 128 : t * 128 + 128], part[:, 256 + t * 128 : 384 + t * 128]
                        to_row = ((2 * y + c) * 2 + t) * 16
                        columns[to_row : to_row + 16, lanes] = jnp.concatenate([early, late], axis=0).astype(jnp.bfloat16)

    copy.wait()
    for n in range(4):
        total = jnp.dot(columns[...], weights[:, n * 256 : (n + 1) * 256], preferred_element_type=jnp.float32)
        peak = total[0:16]
        for t in range(1, 16):
            peak = jnp.maximum(peak, total[t * 16 : (t + 1) * 16])
        logs[:, n * 256 : (n + 1) * 256] = jnp.log(jnp.maximum(peak, 0.1))

    row = lax.broadcasted_iota(jnp.int32, (16, 128), 0)
    mine = lane == me_ref[0] * 16 + row
    base = jnp.sum(jnp.where(mine, base_ref[...].astype(jnp.float32), 0.0), axis=1, keepdims=True)
    wet = wet_ref[...].astype(jnp.float32)
    bottom = jnp.log(jnp.full((16, 1), 0.1, jnp.float32))

    @pl.loop(0, NB, unroll=4)
    def _(j):
        log_level = jnp.broadcast_to(bottom + 0.15 * (base + j.astype(jnp.float32)), (16, 128))
        total = jnp.zeros((16, 128), jnp.float32)
        for b in range(8):
            part = slice(b * 128, b * 128 + 128)
            total += rates_ref[:, part] * erfc((log_level - logs[:, part]) * scale)
        sums[pl.ds(pl.multiple_of(j * 16, 16), 16), :] = total

    for j in range(NB):
        hazard = jnp.sum(sums[j * 16 : j * 16 + 16, :], axis=1, keepdims=True) * (0.5 / K)
        out_ref[j : j + 1, :] = jnp.sum(jnp.where(mine, hazard, 0.0), axis=0, keepdims=True) * wet


def hazard_of(me, got, weights, rates, base, wet):
    vmem = pl.BlockSpec(memory_space=pltpu.VMEM)
    return pl.pallas_call(
        hazard_kernel,
        out_shape=jax.ShapeDtypeStruct((16, 128), jnp.float32),
        in_specs=[pl.BlockSpec(memory_space=pltpu.SMEM), vmem, pl.BlockSpec(memory_space=pl.ANY), vmem, vmem, vmem],
        out_specs=vmem,
        scratch_shapes=[
            pltpu.VMEM((256, 2048), jnp.bfloat16),
            pltpu.VMEM((2048, K), jnp.bfloat16),
            pltpu.VMEM((16, 1024), jnp.float32),
            pltpu.VMEM((256, 128), jnp.float32),
            pltpu.SemaphoreType.DMA,
        ],
        compiler_params=pltpu.CompilerParams(vmem_limit_bytes=52 * MIB),
        name="hazard_levels",
    )(me, got, weights, rates, base, wet)


def body(waveforms, scen_weights, rates, tile_cells, level_base, wet_mask):
    me, z = lax.axis_index(("y", "c")), lax.axis_index("z")

    def fetch(steps):
        ring = [(((i + steps[r]) % 16) * 8 + r, i * 8 + r) for i in range(16) for r in range(8)]
        return lax.ppermute(scen_weights.T, ("z", "y", "c"), ring)

    far, near = fetch(FAR), fetch(NEAR)
    far, near, sent = lax.optimization_barrier((far, near, gather(tile_cells, waveforms.reshape(64, C))))
    weights = lax.all_gather(jnp.concatenate([near, far], axis=0), ("x", "y", "c"), axis=0, tiled=True)
    got = lax.all_to_all(sent.reshape(512, 8, 128), EVERY, 0, 0, tiled=True)
    part = hazard_of(
        jnp.stack([me, z]),
        got.reshape(C // 2, 128),
        weights,
        rates.reshape(1, K),
        level_base.reshape(1, 128),
        wet_mask.reshape(1, 128),
    )
    return lax.psum_scatter(part, ("y", "c"), scatter_dimension=0, tiled=True)


def solution(mesh):
    split = Mesh(mesh.devices.reshape(16, 4, 4, 2), EVERY)
    src, tm = ("z", "x"), ("y", "c")
    return jax.shard_map(
        body,
        mesh=split,
        in_specs=(P(tm, src, None), P(None, src), P(), P(), P(src), P(src)),
        out_specs=P(tm, src),
        check_vma=False,
    )
```
